32 devices in a mesh: ctx: 8 (over y, x, core), fsdp: 4 (over z).
Axes of the slice: x: 2, y: 2, z: 4, core: 2. Of those that a mesh axis runs over, the one named last changes fastest.
Arguments:
- activations: bfloat16 [4, 8192, 1088], P('fsdp', 'ctx'), may hold values from -6 to 6
- doc_lengths: int32 [4, 6], P('fsdp'), may hold values from 1 to 8187, as said below
- cotangent: bfloat16 [4, 8192, 1088], P('fsdp', 'ctx'), may hold values from -6 to 6
- attn_gain: float32 [1088], P('fsdp'), may hold values from 0.5 to 1.5
- attn_shift: float32 [1088], P('fsdp'), may hold values from -1.75 to 1.75
- w_qkv: float32 [1088, 3264], P('fsdp'), may hold values from -0.1875 to 0.1875
- query_bias: float32 [1088], P('fsdp'), may hold values from -3 to 3
- value_bias: float32 [1088], P('fsdp'), may hold values from -3 to 3
- w_out: float32 [1088, 1088], P('fsdp'), may hold values from -0.75 to 0.75
- out_bias: float32 [1088], P('fsdp'), may hold values from -1.75 to 1.75
- mlp_gain: float32 [1088], P('fsdp'), may hold values from 0.5 to 1.5
- mlp_shift: float32 [1088], P('fsdp'), may hold values from -1.75 to 1.75
- w_fc: float32 [1088, 4352], P('fsdp'), may hold values from -0.1875 to 0.1875
- fc_bias: float32 [4352], P('fsdp'), may hold values from -1.75 to 1.75
- w_proj: float32 [4352, 1088], P('fsdp'), may hold values from -0.09375 to 0.09375
- proj_bias: float32 [1088], P('fsdp'), may hold values from -1.75 to 1.75
Outputs:
- block_out: bfloat16 [4, 8192, 1088], P('fsdp', 'ctx')
- input_grad: float32 [4, 8192, 1088], P('fsdp', 'ctx')
- attn_gain_grad: float32 [1088], P('fsdp')
- attn_shift_grad: float32 [1088], P('fsdp')
- w_qkv_grad: float32 [1088, 3264], P('fsdp')
- query_bias_grad: float32 [1088], P('fsdp')
- value_bias_grad: float32 [1088], P('fsdp')
- w_out_grad: float32 [1088, 1088], P('fsdp')
- out_bias_grad: float32 [1088], P('fsdp')
- mlp_gain_grad: float32 [1088], P('fsdp')
- mlp_shift_grad: float32 [1088], P('fsdp')
- w_fc_grad: float32 [1088, 4352], P('fsdp')
- fc_bias_grad: float32 [4352], P('fsdp')
- w_proj_grad: float32 [4352, 1088], P('fsdp')
- proj_bias_grad: float32 [1088], P('fsdp')
The draws below stay inside these ranges and needn't reach their ends.
Inputs may be any that keep to these rules, and one draw needn't show every extreme that they name: `doc_lengths`: in each sequence the 6 lengths are positive and sum to 8192; one of them is longer than 7168.
All inputs are finite; a program needn't handle non-finite values.
Results may differ from the reference program's by a relative error of at most 0.014.
The reference program's roundings to bfloat16 on the way count: a program that leaves them out, or rounds other values in their place, can miss the bound.
Values may be sent and summed in bfloat16 or wider, within the bound.
A program may use at most 448 MiB of HBM per device.

```python
import math
import jax
import jax.numpy as jnp
from jax import lax

D = 1088
HEADS = 17
HEAD = 64
FF = 4352
WINDOW = 1024
DOCS = 6
TOK_DEV = 1024
SEQ = 8192
SEQS = 4


def draw_doc_lengths(key, part):
    key = jax.random.fold_in(key, 11)
    small_key, place_key = jax.random.split(key)
    small = jax.random.randint(small_key, (SEQS, DOCS), 1, TOK_DEV // DOCS + 1)
    row = jnp.arange(SEQS)[:, None]
    small = jnp.where(row == 0, 1, small)
    chosen = jax.random.randint(place_key, (SEQS, 1), 0, DOCS)
    column = jnp.arange(DOCS)[None, :]
    others = jnp.sum(jnp.where(column == chosen, 0, small), axis=1, keepdims=True)
    return jnp.where(column == chosen, SEQ - others, small).astype(jnp.int32)


def block_scale(key, dims, shards, smallest, largest):
    factor_of = 1.0
    for dim, shards_of in shards:
        draws = jax.random.uniform(jax.random.fold_in(jax.random.fold_in(key, 6), dim), (shards_of,), jnp.float32, smallest / len(shards), largest / len(shards))
        factor_of = factor_of * jnp.repeat(jnp.exp(draws), dims[dim] // shards_of).reshape((-1,) + (1,) * (len(dims) - 1 - dim))
    return factor_of


def normal_values(rng, shape, deviation, limit, cuts=(), kind=jnp.bfloat16):
    values = deviation * jax.random.normal(rng, shape, jnp.float32)
    if cuts:
        values = values * block_scale(rng, shape, cuts, -0.22, 0.18)
    return jnp.clip(values, -limit, limit).astype(kind)


def setup_inputs(seed: int = 0) -> dict:
    arg_keys = jax.random.split(jax.random.key(seed), 17)
    return {
        "activations": normal_values(arg_keys[0], (SEQS, SEQ, D), 1.0, 6.0, ((0, 4), (1, 8))),
        "doc_lengths": draw_doc_lengths(jax.random.fold_in(arg_keys[16], 71), 0),
        "cotangent": normal_values(arg_keys[2], (SEQS, SEQ, D), 1.0, 6.0, ((0, 4), (1, 8))),
        "attn_gain": jnp.clip(1.0 + 0.1 * jax.random.normal(arg_keys[3], (D,), jnp.float32), 0.5, 1.5),
        "attn_shift": normal_values(arg_keys[4], (D,), 0.3, 1.75, ((0, 4),), jnp.float32),
        "w_qkv": normal_values(arg_keys[5], (D, 3 * D), D ** -0.5, 0.1875, ((0, 4),), jnp.float32),
        "query_bias": normal_values(arg_keys[6], (D,), 0.5, 3.0, ((0, 4),), jnp.float32),
        "value_bias": normal_values(arg_keys[7], (D,), 0.5, 3.0, ((0, 4),), jnp.float32),
        "w_out": normal_values(arg_keys[8], (D, D), (D // 16) ** -0.5, 0.75, ((0, 4),), jnp.float32),
        "out_bias": normal_values(arg_keys[9], (D,), 0.3, 1.75, ((0, 4),), jnp.float32),
        "mlp_gain": jnp.clip(1.0 + 0.1 * jax.random.normal(arg_keys[10], (D,), jnp.float32), 0.5, 1.5),
        "mlp_shift": normal_values(arg_keys[11], (D,), 0.3, 1.75, ((0, 4),), jnp.float32),
        "w_fc": normal_values(arg_keys[12], (D, FF), D ** -0.5, 0.1875, ((0, 4),), jnp.float32),
        "fc_bias": normal_values(arg_keys[13], (FF,), 0.3, 1.75, ((0, 4),), jnp.float32),
        "w_proj": normal_values(arg_keys[14], (FF, D), FF ** -0.5, 0.09375, ((0, 4),), jnp.float32),
        "proj_bias": normal_values(arg_keys[15], (D,), 0.3, 1.75, ((0, 4),), jnp.float32),
    }


@jax.custom_vjp
def low(v):
    return lax.optimization_barrier(v.astype(jnp.bfloat16)).astype(jnp.float32)

@jax.custom_vjp
def low_back(v):
    return v

def low_keep(v):
    return (low(v), None)

def low_pass(kept, grad):
    return (grad,)

def back_keep(v):
    return (v, None)

def back_low(kept, grad):
    return (low(grad),)
low.defvjp(low_keep, low_pass)
low_back.defvjp(back_keep, back_low)
epsilon = 1e-05
masked_score = -1e+30

def layer_norm(values, gain, shift):
    middle = lax.optimization_barrier(jnp.mean(values, axis=-1, keepdims=True))
    centred = values - middle
    spread = lax.optimization_barrier(jnp.mean(centred * centred, axis=-1, keepdims=True))
    return centred * lax.rsqrt(spread + epsilon) * gain + shift

def segment_ids(lengths_row, positions):
    ends = jnp.cumsum(lengths_row).astype(jnp.int32)
    found = lax.optimization_barrier(jnp.sum((positions[:, None] >= ends[None, :]).astype(jnp.int32), axis=1)).astype(jnp.int32)
    return jnp.where(positions >= 0, found, -1).astype(jnp.int32)

def attend(queries, keys, values, lengths_row):
    length = queries.shape[0]
    block_rows = min(512, length)
    padding = jnp.zeros((WINDOW,) + keys.shape[1:], jnp.float32)
    keys_ext = jnp.concatenate([padding, keys], axis=0)
    values_ext = jnp.concatenate([padding, values], axis=0)
    score_scale = 1.0 / math.sqrt(HEAD)

    def one_block(index):
        first = (index * block_rows).astype(jnp.int32)
        query_pos = first + jnp.arange(block_rows, dtype=jnp.int32)
        key_pos = first - WINDOW + jnp.arange(block_rows + WINDOW, dtype=jnp.int32)
        distance = query_pos[:, None] - key_pos[None, :]
        same_doc = segment_ids(lengths_row, query_pos)[:, None] == segment_ids(lengths_row, key_pos)[None, :]
        allowed = (distance >= 0) & (distance <= WINDOW) & same_doc
        query_block = lax.dynamic_slice_in_dim(queries, first, block_rows, 0)
        key_block = lax.dynamic_slice_in_dim(keys_ext, first, block_rows + WINDOW, 0)
        value_block = lax.dynamic_slice_in_dim(values_ext, first, block_rows + WINDOW, 0)
        scores = jnp.einsum('qhe,khe->hqk', query_block, key_block, precision=lax.Precision.HIGHEST) * score_scale
        scores = low_back(scores)
        probability = jax.nn.softmax(jnp.where(allowed[None], scores, masked_score), axis=-1)
        mixed = jnp.einsum('hqk,khe->qhe', low(probability), value_block, precision=lax.Precision.HIGHEST)
        return mixed.reshape(block_rows, -1)
    outputs = lax.map(jax.checkpoint(one_block), jnp.arange(length // block_rows, dtype=jnp.int32))
    return outputs.reshape(length, -1)

def forward(params, tokens, lengths_row):
    lowered = [low(item) for item in params]
    gain_one, shift_one, w_qkv, query_bias, value_bias, w_out, out_bias = lowered[:7]
    gain_two, shift_two, w_fc, fc_bias, w_proj, proj_bias = lowered[7:]
    length = tokens.shape[0]
    highest = lax.Precision.HIGHEST
    normed = low(layer_norm(tokens, gain_one, shift_one))
    bias_all = jnp.concatenate([query_bias, jnp.zeros_like(query_bias), value_bias])
    qkv = low(low_back(jnp.dot(normed, w_qkv, precision=highest) + bias_all))
    queries = qkv[:, :D].reshape(length, HEADS, HEAD)
    keys = qkv[:, D:2 * D].reshape(length, HEADS, HEAD)
    values = qkv[:, 2 * D:].reshape(length, HEADS, HEAD)
    attended = low(low_back(attend(queries, keys, values, lengths_row)))
    resid = tokens + low_back(jnp.dot(attended, w_out, precision=highest) + out_bias)
    hidden = low(layer_norm(resid, gain_two, shift_two))
    pre_act = low_back(jnp.dot(hidden, w_fc, precision=highest) + fc_bias)
    activated = low(jax.nn.gelu(pre_act, approximate=True))
    return resid + low_back(jnp.dot(activated, w_proj, precision=highest) + proj_bias)

def reference(activations, doc_lengths, cotangent, attn_gain, attn_shift, w_qkv, query_bias, value_bias, w_out, out_bias, mlp_gain, mlp_shift, w_fc, fc_bias, w_proj, proj_bias):
    params = (attn_gain, attn_shift, w_qkv, query_bias, value_bias, w_out, out_bias, mlp_gain, mlp_shift, w_fc, fc_bias, w_proj, proj_bias)

    def one_sequence(summed, item):
        seq_tokens, seq_lengths, seq_cot = item

        def apply_layer(weights, tokens):
            return forward(weights, tokens, seq_lengths)
        result, pull = jax.vjp(apply_layer, params, seq_tokens.astype(jnp.float32))
        weight_grads, token_grad = pull(seq_cot.astype(jnp.float32))
        summed = jax.tree.map(jnp.add, summed, weight_grads)
        return (summed, (result.astype(jnp.bfloat16), token_grad))
    zeros = jax.tree.map(jnp.zeros_like, params)
    summed, stacked = lax.scan(one_sequence, zeros, (activations, doc_lengths, cotangent))
    return (stacked[0], stacked[1], summed[0], summed[1], summed[2], summed[3], summed[4], summed[5], summed[6], summed[7], summed[8], summed[9], summed[10], summed[11], summed[12])
```

```python
import math

import jax
import jax.numpy as jnp
from jax import lax
from jax.experimental import pallas as pl
from jax.experimental.pallas import tpu as pltpu
from jax.sharding import PartitionSpec as P

HEAD = 64
WINDOW = 1024
TILE = 128
ROWS = 256
LOG2E = 1.4426950408889634
epsilon = 1e-05
masked_score = -1e30
VMEM_BYTES = 60 * 1024 * 1024

NT = (((1,), (1,)), ((), ()))
TN = (((0,), (0,)), ((), ()))


def dot_f32(left, right, dims=(((1,), (0,)), ((), ()))):
    return lax.dot_general(left, right, dims, preferred_element_type=jnp.float32)


def head_lanes(rows, which):
    lane = lax.broadcasted_iota(jnp.int32, (rows, TILE), 1)
    return lane < HEAD if which == 0 else lane >= HEAD


def attention_forward_kernel(
    last, tok, q_ref, kh_ref, ko_ref, vh_ref, vo_ref, qdoc_ref, kdoc_ref,
    low_ref, full_ref, stat_ref, kcat, vcat,
):
    pair = pl.program_id(0)
    scale2 = LOG2E / math.sqrt(HEAD)
    span = ROWS + WINDOW

    @pl.when(pair == 0)
    def _():
        kcat[:, TILE:] = kdoc_ref[...]
        stat_ref[...] = jnp.zeros_like(stat_ref)

    kcat[:WINDOW, :TILE] = kh_ref[...]
    kcat[WINDOW:, :TILE] = ko_ref[...]
    vcat[:WINDOW] = vh_ref[...]
    vcat[WINDOW:] = vo_ref[...]
    row = lax.broadcasted_iota(jnp.int32, (ROWS, ROWS), 0)
    col = lax.broadcasted_iota(jnp.int32, (ROWS, ROWS), 1)
    lane = lax.broadcasted_iota(jnp.int32, (ROWS, TILE), 1)

    def one(block, which):
        rows = pl.ds(block * ROWS, ROWS)
        keys = pl.ds(block * ROWS, span)
        query = q_ref[rows, :]
        query = jnp.where(head_lanes(ROWS, which), query, jnp.zeros_like(query))
        query = jnp.concatenate([query, qdoc_ref[rows, :]], axis=1)
        scores = dot_f32(query, kcat[keys, :], NT)
        first = jnp.where(col >= row, scores[:, :ROWS], masked_score)
        final = jnp.where(col <= row, scores[:, WINDOW:], masked_score)
        scores = jnp.concatenate([first, scores[:, ROWS:WINDOW], final], axis=1)
        top = jnp.max(scores, axis=1, keepdims=True)
        expo = jnp.exp2((scores - top) * scale2)
        total = jnp.sum(expo, axis=1, keepdims=True)
        mixed = dot_f32(expo.astype(jnp.bfloat16), vcat[keys, :])
        stat = top * scale2 + jnp.log2(total)
        stat_ref[rows, :] = jnp.where(lane == 2 * pair + which, stat, stat_ref[rows, :])
        return mixed / total

    def block_out(heads):
        for block in range(tok // ROWS):
            rows = pl.ds(block * ROWS, ROWS)
            mixed = one(block, 0)
            other = one(block, 1) if heads == 2 else jnp.zeros_like(mixed)
            mixed = jnp.where(head_lanes(ROWS, 0), mixed, other)
            low_ref[rows, :] = mixed.astype(jnp.bfloat16)
            full_ref[rows, :] = mixed

    if last is None:
        block_out(2)
    else:
        pl.when(pair < last)(lambda: block_out(2))
        pl.when(pair == last)(lambda: block_out(1))


def attention_backward_kernel(
    last, tok, back, q_ref, kh_ref, ko_ref, vh_ref, vo_ref, do_ref, full_ref, lse_ref,
    qdoc_ref, kdoc_ref, dq_ref, dko_ref, dvo_ref,
    kcat, vcat, dk_acc, dv_acc, delta_ref,
):
    pair = pl.program_id(0)
    scale = 1.0 / math.sqrt(HEAD)
    scale2 = LOG2E * scale
    span = ROWS + WINDOW

    @pl.when(pair == 0)
    def _():
        kcat[:, TILE:] = kdoc_ref[...]

    kcat[:WINDOW, :TILE] = kh_ref[...]
    kcat[WINDOW:, :TILE] = ko_ref[...]
    vcat[:WINDOW] = vh_ref[...]
    vcat[WINDOW:] = vo_ref[...]
    dk_acc[...] = jnp.zeros_like(dk_acc)
    dv_acc[...] = jnp.zeros_like(dv_acc)
    key = lax.broadcasted_iota(jnp.int32, (ROWS, ROWS), 0)
    qry = lax.broadcasted_iota(jnp.int32, (ROWS, ROWS), 1)
    valid = head_lanes(tok, 0) | (pair < last if last is not None else True)
    product = jnp.where(valid, do_ref[...].astype(jnp.float32) * full_ref[...], 0.0)
    pick_row = lax.broadcasted_iota(jnp.int32, (8, TILE), 0)
    pick_lane = lax.broadcasted_iota(jnp.int32, (8, TILE), 1)
    pick = (pick_row == pick_lane // HEAD).astype(jnp.float32)
    delta_ref[...] = lax.dot_general(
        pick, product, NT, precision=lax.Precision.HIGHEST, preferred_element_type=jnp.float32
    )

    def one(block, which):
        rows = pl.ds(block * ROWS, ROWS)
        keys = pl.ds(block * ROWS, span)
        lanes = head_lanes(ROWS, which)
        query = q_ref[rows, :]
        query = jnp.where(lanes, query, jnp.zeros_like(query))
        upstream = do_ref[rows, :]
        upstream = jnp.where(lanes, upstream, jnp.zeros_like(upstream))
        query_doc = jnp.concatenate([query, qdoc_ref[rows, :]], axis=1)
        scores = dot_f32(kcat[keys, :], query_doc, NT)
        first = jnp.where(key >= qry, scores[:ROWS], masked_score)
        final = jnp.where(key <= qry, scores[WINDOW:], masked_score)
        scores = jnp.concatenate([first, scores[ROWS:WINDOW], final], axis=0)
        stat = lse_ref[0, which : which + 1, rows]
        delta = delta_ref[which : which + 1, rows]
        prob = jnp.exp2(scores * scale2 - stat)
        dprob = dot_f32(vcat[keys, :], upstream, NT)
        dscore = (prob * (dprob - delta)).astype(jnp.bfloat16)
        dv_acc[keys, :] += dot_f32(prob.astype(jnp.bfloat16), upstream)
        dk_acc[keys, :] += dot_f32(dscore, query)
        lanes_k = head_lanes(span, which)
        keys_one = kcat[keys, :TILE]
        keys_one = jnp.where(lanes_k, keys_one, jnp.zeros_like(keys_one))
        return dot_f32(dscore, keys_one, TN)

    def block_out(heads):
        for block in range(tok // ROWS):
            rows = pl.ds(block * ROWS, ROWS)
            dq = one(block, 0)
            if heads == 2:
                dq = dq + one(block, 1)
            dq_ref[rows, :] = (dq * scale).astype(jnp.bfloat16)

    if last is None:
        block_out(2)
    else:
        pl.when(pair < last)(lambda: block_out(2))
        pl.when(pair == last)(lambda: block_out(1))
    back.buf[pair, 0] = (dk_acc[:WINDOW] * scale).astype(jnp.bfloat16)
    back.buf[pair, 1] = dv_acc[:WINDOW].astype(jnp.bfloat16)
    back.send(pair)
    dko_ref[...] = (dk_acc[WINDOW:] * scale).astype(jnp.bfloat16)
    dvo_ref[...] = dv_acc[WINDOW:].astype(jnp.bfloat16)


def attention_forward(qkv, halo, qdoc, kdoc, features, engine, ident):
    tok = qkv.shape[0]
    pairs = -(-features // TILE)
    heads = features // HEAD
    last = pairs - 1 if heads % 2 else None
    blk = lambda off: pl.BlockSpec((tok, TILE), lambda p, off=off: (0, off + p))
    halo_blk = lambda off: pl.BlockSpec((WINDOW, TILE), lambda p, off=off: (0, off + p))
    fixed = lambda rows: pl.BlockSpec((rows, TILE), lambda p: (0, 0))
    return fused_call(
        lambda *refs: attention_forward_kernel(last, tok, *refs),
        pairs,
        (qkv, halo, qkv, halo, qkv, qdoc, kdoc),
        [
            blk(0), halo_blk(0), blk(pairs), halo_blk(pairs), blk(2 * pairs),
            fixed(tok), fixed(tok + WINDOW),
        ],
        [blk(0), blk(0), fixed(tok)],
        [
            jax.ShapeDtypeStruct((tok, features), jnp.bfloat16),
            jax.ShapeDtypeStruct((tok, pairs * TILE), jnp.float32),
            jax.ShapeDtypeStruct((tok, TILE), jnp.float32),
        ],
        [
            pltpu.VMEM((tok + WINDOW, 2 * TILE), jnp.bfloat16),
            pltpu.VMEM((tok + WINDOW, TILE), jnp.bfloat16),
        ],
        [engine],
        *gather_plan(engine, pairs),
        ident,
        cost=pl.CostEstimate(
            flops=4 * heads * tok * (ROWS + WINDOW) * HEAD * 4,
            bytes_accessed=tok * features * 20,
            transcendentals=heads * tok * (ROWS + WINDOW),
        ),
    )


def attention_backward(
    qkv, halo, upstream, full, lse, qdoc, kdoc, features, reduce, share, ident
):
    tok = qkv.shape[0]
    pairs = -(-features // TILE)
    heads = features // HEAD
    last = pairs - 1 if heads % 2 else None
    blk = lambda off: pl.BlockSpec((tok, TILE), lambda p, off=off: (0, off + p))
    halo_blk = lambda off: pl.BlockSpec((WINDOW, TILE), lambda p, off=off: (0, off + p))
    fixed = lambda rows: pl.BlockSpec((rows, TILE), lambda p: (0, 0))
    wide = pairs * TILE
    back = HaloBack(pairs, wide)
    schedule, end, done = reduce_plan(reduce, pairs, pairs - 3)
    those = range(len(share.jobs))
    schedule[3] += [call(lambda j: share.fetch(j).start(), j) for j in those]
    schedule[4] += [share.both(share.start, j) for j in those]
    schedule[7] += [share.both(share.across, j) for j in those]
    end += done + [share.both(share.finish, j) for j in those] + [back.finish]
    return fused_call(
        lambda *refs: attention_backward_kernel(last, tok, back, *refs),
        pairs,
        (qkv, halo, qkv, halo, qkv, upstream, full, lse, qdoc, kdoc),
        [
            blk(0), halo_blk(0), blk(pairs), halo_blk(pairs), blk(2 * pairs),
            blk(0), blk(0), pl.BlockSpec((1, 2, tok), lambda p: (p, 0, 0)),
            fixed(tok), fixed(tok + WINDOW),
        ],
        [blk(0), blk(0), blk(0)],
        [
            jax.ShapeDtypeStruct((tok, wide), jnp.bfloat16),
            jax.ShapeDtypeStruct((tok, wide), jnp.bfloat16),
            jax.ShapeDtypeStruct((tok, wide), jnp.bfloat16),
        ],
        [
            pltpu.VMEM((tok + WINDOW, 2 * TILE), jnp.bfloat16),
            pltpu.VMEM((tok + WINDOW, TILE), jnp.bfloat16),
            pltpu.VMEM((tok + WINDOW, TILE), jnp.float32),
            pltpu.VMEM((tok + WINDOW, TILE), jnp.float32),
            pltpu.VMEM((8, tok), jnp.float32),
        ],
        [reduce, share, back],
        schedule,
        end,
        ident,
        chain=True,
        cost=pl.CostEstimate(
            flops=10 * heads * tok * (ROWS + WINDOW) * HEAD * 4,
            bytes_accessed=tok * features * 40,
            transcendentals=heads * tok * (ROWS + WINDOW),
        ),
    )


GELU_A = math.sqrt(2.0 / math.pi)
GELU_B = 0.044715


def mlp_kernel(
    steps, opening, norm_ref, normt_ref, cot_ref, cott_ref, base_ref, dbase_ref, pbias_ref, fc_ref, fcb_ref, proj_ref,
    out_ref, dnorm_ref, gproj_ref, gfc_ref, gfcb_ref, final_acc, act_s, dpre_s,
):
    step = pl.program_id(0)
    tok = norm_ref.shape[0]

    @pl.when(step == 0)
    def _():
        final_acc[...] = base_ref[...]
        dnorm_ref[...] = jnp.zeros_like(dnorm_ref) if opening else dbase_ref[...]

    bias_sum = jnp.zeros(gfcb_ref.shape, jnp.float32)
    for part in range(tok // ROWS):
        rows = pl.ds(part * ROWS, ROWS)
        pre = dot_f32(norm_ref[rows, :], fc_ref[...]) + fcb_ref[...]
        dact = dot_f32(cot_ref[rows, :], proj_ref[...], NT)
        square = pre * pre
        bent = jnp.tanh(GELU_A * pre * (1.0 + GELU_B * square))
        half = 0.5 * (1.0 + bent)
        act = (pre * half).astype(jnp.bfloat16)
        slope = half + 0.5 * pre * (1.0 - bent * bent) * (
            GELU_A * (1.0 + 3.0 * GELU_B * square)
        )
        dpre = (dact * slope).astype(jnp.bfloat16)
        act_s[rows, :] = act
        dpre_s[rows, :] = dpre
        bias_sum = bias_sum + jnp.sum(dpre.astype(jnp.float32), axis=0, keepdims=True)
        final_acc[rows, :] += dot_f32(act, proj_ref[...])
        dnorm_ref[rows, :] += dot_f32(dpre, fc_ref[...], NT)
    gfcb_ref[...] = bias_sum
    gproj_ref[...] = dot_f32(cott_ref[...], act_s[...]).T.astype(jnp.bfloat16)
    gfc_ref[...] = dot_f32(normt_ref[...], dpre_s[...]).astype(jnp.bfloat16)

    if not opening:

        @pl.when(step == steps - 1)
        def _():
            for at in range(0, tok, ROWS):
                done = final_acc[at : at + ROWS, :] + pbias_ref[...]
                out_ref[:, at : at + ROWS] = done.T.astype(jnp.bfloat16)


def mlp_part(norm, norm_t, cot, cot_t, base, dbase, pbias, fc_w, fcb, proj_w, engine, schedule, end, ident):
    tok, features = norm.shape
    hidden = fc_w.shape[1]
    width = 256
    steps = hidden // width
    opening = dbase is None
    whole = lambda shape: pl.BlockSpec(shape, lambda j: (0, 0), pipeline_mode=pl.Buffered(1))
    cols = lambda rows: pl.BlockSpec((rows, width), lambda j: (0, j))
    rows = pl.BlockSpec((width, features), lambda j: (j, 0))

    def kern(*refs):
        refs = list(refs)
        if opening:
            refs.insert(5, None)
            refs.insert(6, None)
            refs.insert(15, refs[10])
        mlp_kernel(steps, opening, *refs)

    extra = [] if opening else [pltpu.VMEM((tok, features), jnp.float32)]
    return fused_call(
        kern,
        steps,
        (norm, norm_t, cot, cot_t, base) + (() if opening else (dbase, pbias)) + (fc_w, fcb, proj_w),
        [whole((tok, features)), whole((features, tok))] * 2
        + [whole((tok, features))] * (1 if opening else 2)
        + ([] if opening else [whole((1, features))])
        + [cols(features), cols(1), rows],
        [
            whole((tok, features) if opening else (features, tok)), whole((tok, features)), rows,
            cols(features), cols(1),
        ],
        [
            jax.ShapeDtypeStruct((tok, features), jnp.float32)
            if opening else jax.ShapeDtypeStruct((features, tok), jnp.bfloat16),
            jax.ShapeDtypeStruct((tok, features), jnp.float32),
            jax.ShapeDtypeStruct((hidden, features), jnp.bfloat16),
            jax.ShapeDtypeStruct((features, hidden), jnp.bfloat16),
            jax.ShapeDtypeStruct((1, hidden), jnp.float32),
        ],
        extra
        + [pltpu.VMEM((tok, width), jnp.bfloat16), pltpu.VMEM((tok, width), jnp.bfloat16)],
        [engine],
        schedule,
        end,
        ident,
        cost=pl.CostEstimate(
            flops=12 * tok * features * hidden,
            bytes_accessed=features * hidden * 8 + tok * features * 20,
            transcendentals=tok * hidden,
        ),
    )


def last_kernel(
    reduce, early, late, small, dims, normt_ref, xt_ref, gain_ref, dq_hbm, dk_hbm, dv_hbm, back_hbm, w_hbm,
    gresid_hbm, gout_hbm, fin_a, fin_b, small_hbm, out_hbm, rqkv_hbm, rout_hbm, ra_hbm, rb_hbm,
    small_out,
    g, back, w, resid, full, sums, column, sem_in, sem_out, *refs,
):
    features, tok, shards, wide = dims
    low = jnp.bfloat16
    own = []
    for engine in (reduce, early, late, small):
        own.append(refs[: len(engine.scratch)])
        refs = refs[len(engine.scratch) :]
    reduce.bind([full, gout_hbm], [], own[0])
    early.bind([fin_a, fin_b], [ra_hbm, rb_hbm], own[1])
    late.bind([], [rqkv_hbm, rout_hbm], own[2])
    small.bind([small_hbm], [small_out], own[3])
    ctx, last = lax.axis_index("ctx"), lax.axis_size("ctx") - 1
    loads = [
        pltpu.make_async_copy(src, dst, sem_in.at[n])
        for n, (src, dst) in enumerate((
            (dq_hbm, g.at[:, pl.ds(0, wide)]), (dk_hbm, g.at[:, pl.ds(wide, wide)]),
            (dv_hbm, g.at[:, pl.ds(2 * wide, wide)]), (back_hbm, back), (w_hbm, w),
            (gresid_hbm, resid),
        ))
    ]
    for item in loads:
        item.start()
    for j in (0, 1):
        early.fetch(j).start()
    small.load().start()
    sums[...] = jnp.zeros_like(sums)
    if g.shape[1] > 3 * wide:
        g[:, 3 * wide :] = jnp.zeros_like(g[:, 3 * wide :])
    greet()
    do = lambda action, *given: reduce.both(action, *given)()
    share = lambda engine, action, *given: engine.both(action, *given)()
    for s in range(shards):
        do(reduce.a_start, 1, s)
    for j in (0, 1):
        share(early, early.start, j)
    for item in loads[:4]:
        item.wait()

    @pl.when(ctx < last)
    def _():
        for at in range(0, tok, ROWS):
            some = slice(at, at + ROWS)
            for n in range(back.shape[0]):
                lanes = slice(wide + n * TILE, wide + (n + 1) * TILE)
                total = g[some, lanes].astype(jnp.float32) + back[n, some].astype(jnp.float32)
                g[some, lanes] = total.astype(low)

    def multiply(s):
        full[s] = dot_f32(normt_ref[reduce.owner(s)], g[...]).astype(low)
        do(reduce.a_start, 0, s)

    def columns():
        total = jnp.zeros((1, g.shape[1]), jnp.float32)
        for at in range(0, tok, ROWS):
            part = g[at : at + ROWS].astype(jnp.float32)
            total = total + jnp.sum(part, axis=0, keepdims=True)
        column[0:1] = total[:, :features]
        column[1:2] = total[:, 2 * wide : 2 * wide + features]

    def back_block(block):
        some = pl.ds(block * ROWS, ROWS)
        up = dot_f32(w[...], g[some, :], NT)
        x = xt_ref[:, some].astype(jnp.float32)
        centred = x - jnp.mean(x, axis=0, keepdims=True)
        inverse = lax.rsqrt(jnp.mean(centred * centred, axis=0, keepdims=True) + epsilon)
        hat = centred * inverse
        sums[:, 0:1] += jnp.sum(up * hat, axis=1, keepdims=True)
        sums[:, 1:2] += jnp.sum(up, axis=1, keepdims=True)
        up = up * gain_ref[...]
        lean = jnp.mean(up, axis=0, keepdims=True)
        tilt = jnp.mean(up * hat, axis=0, keepdims=True)
        resid[:, some] = resid[:, some] + inverse * (up - lean - hat * tilt)
        item = pltpu.make_async_copy(
            resid.at[:, some], out_hbm.at[:, some], sem_out.at[block]
        )
        item.start()
        return item

    multiply(0)
    for s in range(shards):
        do(reduce.b_start, 1, s)
    multiply(1)
    do(reduce.b_start, 0, 0)
    multiply(2)
    do(reduce.b_start, 0, 1)
    do(reduce.b_next, 1, 0)
    do(reduce.b_next, 1, 1)
    for s in range(3, shards):
        multiply(s)
    do(reduce.b_start, 0, 2)
    do(reduce.b_next, 0, 0)
    for s in range(2, shards):
        do(reduce.b_next, 1, s)
    for item in loads[4:]:
        item.wait()
    columns()
    for j in (0, 1):
        share(early, early.across, j)
    for s in range(3, shards):
        do(reduce.b_start, 0, s)
    saves = [back_block(0)]
    do(reduce.b_next, 0, 1)
    for s in range(shards):
        do(reduce.c_start, 1, s)
    saves.append(back_block(1))
    for s in range(2, shards):
        do(reduce.b_next, 0, s)
    do(reduce.c_start, 0, 0)
    saves.append(back_block(2))
    do(reduce.c_start, 0, 1)
    do(reduce.total, 1)
    share(late, late.start, 1)
    for block in range(3, tok // ROWS):
        saves.append(back_block(block))
    small.load().wait()
    small.own[0, 0:2] = sums[...].T[0:2]
    small.own[0, 2:4] = column[0:2]
    small.send(0)
    for s in range(2, shards):
        do(reduce.c_start, 0, s)
    small.add(0)
    small.send(1)
    do(reduce.total, 0)
    share(late, late.start, 0)
    small.add(1)
    small.send(2)
    share(late, late.across, 1)
    share(late, late.across, 0)
    small.add(2)
    small.finish()
    for j in (0, 1):
        share(early, early.finish, j)
        share(late, late.finish, j)
        do(reduce.finish, j)
    for item in saves:
        item.wait()


def last_call(
    jobs, early, normt, x_t, gain, dq, dk, dv, back, weights, gresid_t, gout, small, ident
):
    features, tok = x_t.shape
    shards = sizes()[1]
    wide, qkv_wide = dq.shape[1], weights.shape[1]
    low, struct = jnp.bfloat16, jax.ShapeDtypeStruct
    rows = features // shards
    reduce = ReduceHere(jobs, [struct((shards, rows, qkv_wide), low), gout], keep=False)
    late, tiny = Share(jobs, [], reduce), Small(small)
    vm = pl.BlockSpec(memory_space=pltpu.VMEM)
    dma = pltpu.SemaphoreType.DMA
    return pl.pallas_call(
        lambda *refs: last_kernel(
            reduce, early, late, tiny, (features, tok, shards, wide), *refs
        ),
        in_specs=[vm] * 3 + [any_spec()] * 10,
        out_specs=[any_spec()] * 6,
        out_shape=[struct((features, tok), jnp.float32)] + late.outs + early.outs + tiny.outs,
        scratch_shapes=[
            pltpu.VMEM((tok, qkv_wide), low), pltpu.VMEM(back.shape, low),
            pltpu.VMEM((features, qkv_wide), low), pltpu.VMEM((features, tok), jnp.float32),
            pltpu.VMEM((shards, rows, qkv_wide), low), pltpu.VMEM((features, TILE), jnp.float32),
            pltpu.VMEM((8, features), jnp.float32), dma((6,)), dma((tok // ROWS,)),
        ] + reduce.scratch + early.scratch + late.scratch + tiny.scratch,
        compiler_params=pltpu.CompilerParams(
            vmem_limit_bytes=VMEM_BYTES, collective_id=ident, has_side_effects=True
        ),
    )(
        normt.reshape(shards, rows, tok), x_t, gain, dq, dk, dv, back, weights, gresid_t, gout,
        *early.arrays, small,
    )


def at_step(schedule, end, steps, when, action):
    if when < steps:
        schedule.setdefault(when, []).append(action)
    else:
        end.append(action)


def gather_plan(engine, steps, deep=3):
    schedule, end = {0: [engine.open]}, []
    units = engine.units
    for unit in units[:deep]:
        schedule[0].append(engine.both(engine.start, *unit))
    count = len(units)
    late = []
    at_step(schedule, end, steps, 1, engine.keep)
    for n, unit in enumerate(units):
        when = 2 + n * (steps - 4) // count
        at_step(schedule, end, steps, when, engine.both(engine.spread, *unit))
        if n + deep < count:
            at_step(schedule, end, steps, when, engine.both(engine.start, *units[n + deep]))
        late.append((when + 1, engine.both(engine.relay, *unit)))
    for when, action in late:
        at_step(schedule, end, steps, when, action)
    for (when, _), unit in zip(late, units):
        at_step(schedule, end, steps, when + 1, engine.both(engine.across, *unit))
    end += [engine.both(engine.arrived, j) for j in range(len(engine.jobs))]
    end.append(engine.both(engine.close))
    return schedule, end


def reduce_plan(engine, steps, span):
    schedule, end = {}, []
    units = engine.units
    late, later = [], []
    for n, unit in enumerate(units):
        when = n * span // len(units)
        at_step(schedule, end, steps, when, engine.both(engine.a_start, *unit))
        late.append((when + 1, engine.both(engine.b_start, *unit)))
    for when, action in late:
        at_step(schedule, end, steps, when, action)
    for n, unit in enumerate(units):
        at_step(schedule, end, steps, n * span // len(units) + 2, engine.both(engine.b_next, *unit))
    for n, unit in enumerate(units):
        at_step(schedule, end, steps, n * span // len(units) + 3, engine.both(engine.c_start, *unit))
    jobs = range(len(engine.jobs))
    end += [engine.both(engine.total, j) for j in jobs]
    return schedule, end, [engine.both(engine.finish, j) for j in jobs]


def joined(ref, cols):
    shards, rows, _ = ref.shape
    value = ref[:, :, cols]
    if rows % 16:
        value = value.astype(jnp.float32)
    return value.reshape(shards * rows, value.shape[2]).astype(jnp.bfloat16)


def first_kernel(
    engine, dims, xt_ref, ct_ref, wqkv_ref, vec_ref, fc_hbm, proj_hbm, out_hbm,
    qkv_hbm, halo_hbm, normt_hbm, cot_hbm, vfull_ref, wfull_hbm, fca_hbm, fcb_hbm, pa_hbm, pb_hbm,
    outl_hbm, qkv_ref, halo_ref, normt_ref, cot_ref,
    wsrc, vsrc, xh, norm, normh, bias, fc32, proj32, out32, fca_s, fcb_s, pa_s, pb_s, outl_s,
    sem_in, sem_out, sem_x, sem_done, *sems,
):
    features, tok, shards, first, wide, chunk = dims
    low = jnp.bfloat16
    rows = wqkv_ref.shape[0]
    own = proj_hbm.shape[0]
    second = own - first
    parts = (wsrc.shape[1] + chunk - 1) // chunk
    wsrcs, ws, sems = sems[:parts], sems[parts : 2 * parts], sems[2 * parts :]
    engine.bind([vsrc] + list(wsrcs), [vfull_ref] + list(ws), sems)
    ctx, row, last = lax.axis_index("ctx"), lax.axis_index("fsdp"), lax.axis_size("ctx") - 1

    def load(n, src, dst):
        return pltpu.make_async_copy(src, dst, sem_in.at[n])

    cut = fc32.shape[0]
    deep = proj32.shape[0]
    loads = [
        load(0, fc_hbm.at[pl.ds(0, cut)], fc32), load(1, proj_hbm.at[pl.ds(0, deep)], proj32),
        load(2, out_hbm, out32),
    ]
    for item in loads:
        item.start()
    wsrc[...] = jnp.zeros_like(wsrc)
    for n in range(3):
        wsrc[:, n * wide : n * wide + features] = wqkv_ref[
            :, n * features : (n + 1) * features
        ].astype(low)
    vsrc[...] = vec_ref[...].astype(low)
    for n in range(parts):
        wsrcs[n][...] = wsrc[:, n * chunk : min((n + 1) * chunk, wsrc.shape[1])]
    greet(True)
    halo_copy = remote(
        xt_ref, xh, sem_x.at[0], sem_x.at[1], (jnp.minimum(ctx + 1, last), row)
    )
    units = engine.units
    engine.open()
    for unit in units[: shards - 1]:
        engine.both(engine.start, *unit)()
    done = []

    def ready(n, src, dst):
        item = pltpu.make_async_copy(src, dst, sem_done.at[n])
        item.start()
        done.append(item)

    @pl.when(ctx == 0)
    def _():
        xh[...] = jnp.zeros_like(xh)

    saves = [
        pltpu.make_async_copy(src, dst, sem_out.at[n])
        for n, (src, dst) in enumerate(
            ((fca_s, fca_hbm), (fcb_s, fcb_hbm), (pa_s, pa_hbm), (pb_s, pb_hbm),
             (outl_s, outl_hbm))
        )
    ]

    def cast_fc(at):
        load(0, fc_hbm.at[pl.ds(at, cut)], fc32).wait()
        for n in range(shards):
            fca_s[at : at + cut, n * first : (n + 1) * first] = fc32[
                :, n * own : n * own + first
            ].astype(low)
            fcb_s[at : at + cut, n * second : (n + 1) * second] = fc32[
                :, n * own + first : (n + 1) * own
            ].astype(low)
        if at + cut < rows:
            load(0, fc_hbm.at[pl.ds(at + cut, cut)], fc32).start()

    def cast_proj(at):
        load(1, proj_hbm.at[pl.ds(at, deep)], proj32).wait()
        stop = min(max(first - at, 0), deep)
        if stop:
            pa_s[at : at + stop] = proj32[:stop].astype(low)
        if stop < deep:
            pb_s[at + stop - first : at + deep - first] = proj32[stop:].astype(low)
        if at + deep < own:
            load(1, proj_hbm.at[pl.ds(at + deep, deep)], proj32).start()

    def cast_out():
        load(2, out_hbm, out32).wait()
        outl_s[...] = jnp.zeros_like(outl_s)
        outl_s[:, :features] = out32[...].astype(low)
        for item in saves:
            item.start()

    def turn_cot():
        for at in range(0, tok, ROWS):
            cot_ref[at : at + ROWS, :] = ct_ref[:, at : at + ROWS].T
        ready(3, cot_ref, cot_hbm)

    def vectors():
        engine.both(engine.arrived, 0)()
        engine.local(0).wait()
        columns = vfull_ref[...].astype(jnp.float32).reshape(features, vfull_ref.shape[2])
        columns = columns[:, :TILE]
        lines = columns.T
        bias[...] = jnp.zeros_like(bias)
        bias[0:1, :features] = lines[2:3]
        bias[0:1, 2 * wide : 2 * wide + features] = lines[3:4]
        return columns

    def normalise(src, columns, dst, dst_t):
        gain, shift = columns[:, 0:1], columns[:, 1:2]
        for at in range(0, tok, ROWS):
            x = src[:, at : at + ROWS].astype(jnp.float32)
            centred = x - jnp.mean(x, axis=0, keepdims=True)
            spread = jnp.mean(centred * centred, axis=0, keepdims=True)
            y = centred * lax.rsqrt(spread + epsilon) * gain + shift
            if dst_t is not None:
                dst_t[:, at : at + ROWS] = y.astype(low)
            dst[at : at + ROWS, :] = y.T.astype(low)

    def multiply(n):
        engine.both(engine.arrived, 1 + n)()
        engine.local(1 + n).wait()
        lo, hi = n * chunk, min((n + 1) * chunk, wsrc.shape[1])
        weights = joined(ws[n], slice(0, hi - lo))
        item = pltpu.make_async_copy(
            ws[n], wfull_hbm.at[:, :, pl.ds(lo, hi - lo)], sem_done.at[12 + n]
        )
        item.start()
        done.append(item)
        for at in range(0, tok, ROWS):
            part = dot_f32(norm[at : at + ROWS, :], weights) + bias[0:1, lo:hi]
            qkv_ref[at : at + ROWS, lo:hi] = part.astype(low)
        ready(4 + 2 * n, qkv_ref.at[:, pl.ds(lo, hi - lo)], qkv_hbm.at[:, pl.ds(lo, hi - lo)])
        lo_h, hi_h = max(lo, wide), min(hi, 3 * wide)
        if lo_h >= hi_h:
            return
        weights = weights[:, lo_h - lo : hi_h - lo]
        for at in range(0, tok, ROWS):
            part = dot_f32(normh[at : at + ROWS, :], weights) + bias[0:1, lo_h:hi_h]
            halo_ref[at : at + ROWS, lo_h - wide : hi_h - wide] = part.astype(low)
        span = pl.ds(lo_h - wide, hi_h - lo_h)
        ready(5 + 2 * n, halo_ref.at[:, span], halo_hbm.at[:, span])

    per = shards - 1
    groups = [units[n : n + per] for n in range(0, len(units), per)]
    chunks = groups[1:]

    def each(action, group):
        for unit in group:
            engine.both(action, *unit)()

    for group in chunks[:2]:
        each(engine.start, group)
    pl.when(ctx < last)(lambda: halo_copy.start())
    for at in range(0, rows, cut):
        cast_fc(at)
    each(engine.spread, groups[0])
    each(engine.spread, chunks[0])
    for at in range(0, own, deep):
        cast_proj(at)
    cast_out()
    each(engine.relay, groups[0])
    each(engine.relay, chunks[0])
    each(engine.spread, chunks[1])
    each(engine.start, chunks[2])
    turn_cot()
    each(engine.across, groups[0])
    each(engine.across, chunks[0])
    each(engine.relay, chunks[1])
    each(engine.start, chunks[3])
    columns = vectors()
    normalise(xt_ref, columns, norm, normt_ref)
    ready(2, normt_ref, normt_hbm)
    each(engine.spread, chunks[2])
    each(engine.across, chunks[1])
    multiply(0)
    each(engine.spread, chunks[3])
    each(engine.relay, chunks[2])

    @pl.when(ctx > 0)
    def _():
        halo_copy.wait_recv()

    normalise(xh, columns, normh, None)
    each(engine.relay, chunks[3])
    each(engine.across, chunks[2])
    multiply(1)
    each(engine.across, chunks[3])
    multiply(2)
    multiply(3)
    engine.both(engine.close)()
    pl.when(ctx < last)(lambda: halo_copy.wait_send())
    for item in saves + done:
        item.wait()


def first_call(xt, ct, w_qkv, vec, w_fc, w_proj, w_out, first, wide, qkv_wide, out_wide, ident):
    features, tok = xt.shape
    planes, shards = sizes()
    rows, own = w_qkv.shape[0], w_proj.shape[0]
    low = jnp.bfloat16
    chunk = CORES * 4 * TILE
    columns = vec.shape[1]
    struct = jax.ShapeDtypeStruct
    wides = [columns] + [min(chunk, qkv_wide - at) for at in range(0, qkv_wide, chunk)]
    jobs = [best_job(rows, n) for n in wides]
    engine = GatherHere(jobs, [struct((rows, n), low) for n in wides], list(range(len(jobs))))
    dims = features, tok, shards, first, wide, chunk
    vm = pl.BlockSpec(memory_space=pltpu.VMEM)
    second = own - first
    cut = rows // 2 if rows // 2 % 8 == 0 else rows
    dma = pltpu.SemaphoreType.DMA
    return pl.pallas_call(
        lambda *refs: first_kernel(engine, dims, *refs),
        in_specs=[vm] * 4 + [any_spec()] * 3,
        out_specs=[any_spec()] * 4 + [vm] + [any_spec()] * 6,
        out_shape=[
            struct((tok, qkv_wide), low), struct((tok, 2 * wide), low), struct((features, tok), low),
            struct((tok, features), low), struct((shards, rows, columns), low),
            struct((shards, rows, qkv_wide), low), struct((rows, shards * first), low),
            struct((rows, shards * second), low), struct((first, features), low),
            struct((second, features), low), struct((rows, out_wide), low),
        ],
        scratch_shapes=[
            pltpu.VMEM((tok, qkv_wide), low), pltpu.VMEM((tok, 2 * wide), low),
            pltpu.VMEM((features, tok), low), pltpu.VMEM((tok, features), low),
            pltpu.VMEM((rows, qkv_wide), low),
            pltpu.VMEM((rows, columns), low), pltpu.VMEM((features, tok), low),
            pltpu.VMEM((tok, features), low), pltpu.VMEM((tok, features), low),
            pltpu.VMEM((8, qkv_wide), jnp.float32), pltpu.VMEM((cut, w_fc.shape[1]), jnp.float32),
            pltpu.VMEM((own // 2, features), jnp.float32),
            pltpu.VMEM((rows, features), jnp.float32),
            pltpu.VMEM((rows, shards * first), low), pltpu.VMEM((rows, shards * second), low),
            pltpu.VMEM((first, features), low), pltpu.VMEM((second, features), low),
            pltpu.VMEM((rows, out_wide), low), dma((3,)), dma((6,)), dma((2,)),
            dma((16,)),
        ] + [pltpu.VMEM((rows, n), low) for n in wides[1:]]
        + [pltpu.VMEM((shards, rows, n), low) for n in wides[1:]] + engine.scratch,
        compiler_params=pltpu.CompilerParams(
            vmem_limit_bytes=VMEM_BYTES, collective_id=ident, has_side_effects=True
        ),
    )(xt, ct, w_qkv, vec, w_fc, w_proj, w_out)


def final_kernel(
    features, shards, qkv_ref, out_ref, fca_ref, fcb_ref, pa_ref, pb_ref,
    gqkv_ref, gout_ref, gfc_ref, gproj_ref,
):
    step = pl.program_id(0)
    wide = -(-features // TILE) * TILE
    for n in range(3):
        gqkv_ref[:, n * features : (n + 1) * features] = qkv_ref[
            :, n * wide : n * wide + features
        ].astype(jnp.float32)
    gout_ref[...] = out_ref[:, :features].astype(jnp.float32)
    own, first = gfc_ref.shape[1] // shards, fca_ref.shape[1] // shards
    second = own - first
    for n in range(shards):
        gfc_ref[:, n * own : n * own + first] = fca_ref[
            :, n * first : (n + 1) * first
        ].astype(jnp.float32)
        gfc_ref[:, n * own + first : (n + 1) * own] = fcb_ref[
            :, n * second : (n + 1) * second
        ].astype(jnp.float32)
    rows = gproj_ref.shape[0]

    def proj(at):
        stop = min(max(first - at * rows, 0), rows)
        if stop:
            gproj_ref[:stop] = pa_ref[at * rows : at * rows + stop].astype(jnp.float32)
        if stop < rows:
            low = at * rows + stop - first
            gproj_ref[stop:] = pb_ref[low : low + rows - stop].astype(jnp.float32)

    for at in range(own // rows):
        pl.when(step == at)(call(proj, at))


def finals(features, shards, r_qkv, r_out, r_fca, r_fcb, r_proja, r_projb):
    rows, own = r_qkv.shape[0], r_proja.shape[0] + r_projb.shape[0]
    steps = 2 if rows // 2 % 8 == 0 else 1
    blk = lambda a: pl.BlockSpec((rows // steps, a.shape[1]), lambda i: (i, 0))
    whole = lambda a: pl.BlockSpec(a.shape, lambda i: (0, 0), pipeline_mode=pl.Buffered(1))
    shapes = [(rows, 3 * features), (rows, features), (rows, own * shards), (own, features)]
    return pl.pallas_call(
        lambda *refs: final_kernel(features, shards, *refs),
        grid=(steps,),
        in_specs=[blk(a) for a in (r_qkv, r_out, r_fca, r_fcb)]
        + [whole(r_proja), whole(r_projb)],
        out_specs=[pl.BlockSpec((s[0] // steps, s[1]), lambda i: (i, 0)) for s in shapes],
        out_shape=[jax.ShapeDtypeStruct(s, jnp.float32) for s in shapes],
        compiler_params=pltpu.CompilerParams(vmem_limit_bytes=VMEM_BYTES),
    )(r_qkv, r_out, r_fca, r_fcb, r_proja, r_projb)


def out_norm_kernel(att_ref, w_ref, xt_ref, vec_ref, resid_ref, norm_ref, normt_ref):
    features = resid_ref.shape[1]
    mixed = dot_f32(att_ref[...], w_ref[...])[:, :features] + vec_ref[0:1]
    resid = xt_ref[...].astype(jnp.float32).T + mixed
    resid_ref[...] = resid
    centred = resid - jnp.mean(resid, axis=1, keepdims=True)
    spread = jnp.mean(centred * centred, axis=1, keepdims=True)
    normed = centred * lax.rsqrt(spread + epsilon) * vec_ref[1:2] + vec_ref[2:3]
    norm_ref[...] = normed.astype(jnp.bfloat16)
    normt_ref[...] = normed.T.astype(jnp.bfloat16)


def out_norm(attended, out_w, x_t, vec):
    tok, features = attended.shape
    blk = pl.BlockSpec((ROWS, features), lambda i: (i, 0))
    blk_t = pl.BlockSpec((features, ROWS), lambda i: (0, i))
    whole = lambda a: pl.BlockSpec(a.shape, lambda i: (0, 0), pipeline_mode=pl.Buffered(1))
    struct = jax.ShapeDtypeStruct
    return pl.pallas_call(
        out_norm_kernel,
        grid=(tok // ROWS,),
        in_specs=[blk, whole(out_w), blk_t, whole(vec)],
        out_specs=[blk, blk, blk_t],
        out_shape=[
            struct((tok, features), jnp.float32), struct((tok, features), jnp.bfloat16),
            struct((features, tok), jnp.bfloat16),
        ],
        compiler_params=pltpu.CompilerParams(vmem_limit_bytes=VMEM_BYTES),
    )(attended, out_w, x_t, vec)


def middle_kernel(
    steps, dnorm_ref, resid_ref, cot_ref, att_ref, w_ref, vec_ref,
    gresid_ref, datt_ref, gout_ref, sums_ref, branch_t,
):
    step = pl.program_id(0)
    features = resid_ref.shape[1]

    @pl.when(step == 0)
    def _():
        sums_ref[...] = jnp.zeros_like(sums_ref)

    up, resid = dnorm_ref[...], resid_ref[...]
    cot = cot_ref[...].astype(jnp.float32)
    centred = resid - jnp.mean(resid, axis=1, keepdims=True)
    inverse = lax.rsqrt(jnp.mean(centred * centred, axis=1, keepdims=True) + epsilon)
    hat = centred * inverse
    sums_ref[0:1] += jnp.sum(up * hat, axis=0, keepdims=True)
    sums_ref[1:2] += jnp.sum(up, axis=0, keepdims=True)
    sums_ref[3:4] += jnp.sum(cot, axis=0, keepdims=True)
    up = up * vec_ref[1:2]
    lean = jnp.mean(up, axis=1, keepdims=True)
    tilt = jnp.mean(up * hat, axis=1, keepdims=True)
    gresid = cot + inverse * (up - lean - hat * tilt)
    turned = gresid.T
    gresid_ref[...] = turned
    branch = gresid.astype(jnp.bfloat16)
    branch_t[:, pl.ds(pl.multiple_of(step * ROWS, ROWS), ROWS)] = turned.astype(jnp.bfloat16)
    sums_ref[2:3] += jnp.sum(branch.astype(jnp.float32), axis=0, keepdims=True)
    datt_ref[...] = dot_f32(branch, w_ref[:, :features], NT).astype(jnp.bfloat16)

    @pl.when(step == steps - 1)
    def _():
        gout_ref[:, features:] = jnp.zeros_like(gout_ref[:, features:])
        for at in range(0, features, ROWS):
            some = slice(at, min(at + ROWS, features))
            grad = dot_f32(branch_t[some, :], att_ref[...])
            gout_ref[:, some] = grad.T.astype(jnp.bfloat16)


def middle(dnorm, resid, cot, attended, out_w, vec):
    tok, features = resid.shape
    steps = tok // ROWS
    blk = pl.BlockSpec((ROWS, features), lambda i: (i, 0))
    blk_t = pl.BlockSpec((features, ROWS), lambda i: (0, i))
    whole = lambda shape: pl.BlockSpec(shape, lambda i: (0, 0), pipeline_mode=pl.Buffered(1))
    struct = jax.ShapeDtypeStruct
    return pl.pallas_call(
        lambda *refs: middle_kernel(steps, *refs),
        grid=(steps,),
        in_specs=[blk, blk, blk, whole(attended.shape), whole(out_w.shape), whole(vec.shape)],
        out_specs=[blk_t, blk, whole(out_w.shape), whole((8, features))],
        out_shape=[
            struct((features, tok), jnp.float32), struct((tok, features), jnp.bfloat16),
            struct(out_w.shape, jnp.bfloat16), struct((8, features), jnp.float32),
        ],
        scratch_shapes=[pltpu.VMEM((features, tok), jnp.bfloat16)],
        compiler_params=pltpu.CompilerParams(
            vmem_limit_bytes=VMEM_BYTES, fuse_transposed_lhs_in_matmul=True
        ),
    )(dnorm, resid, cot, attended, out_w, vec)


MESH = pl.DeviceIdType.MESH
CORES = 2


def place():
    ctx, row = lax.axis_index("ctx"), lax.axis_index("fsdp")
    planes, shards = lax.axis_size("ctx") // CORES, lax.axis_size("fsdp")
    return ctx // CORES, lax.rem(ctx, CORES), row, planes, shards


def plane_peer(plane, core, row, planes, by):
    return (lax.rem(plane + by, planes) * CORES + core, row)


def greet(chain=False):
    plane, core, row, planes, shards = place()
    ctx = plane * CORES + core
    barrier = pltpu.get_barrier_semaphore()
    if chain:
        last = planes * CORES - 1

        @pl.when(ctx > 0)
        def _():
            pl.semaphore_signal(barrier, inc=1, device_id=(ctx - 1, row), device_id_type=MESH)

        @pl.when(ctx < last)
        def _():
            pl.semaphore_signal(barrier, inc=1, device_id=(ctx + 1, row), device_id_type=MESH)

    peers = [(plane * CORES + 1 - core, row)]
    peers += [plane_peer(plane, core, row, planes, by) for by in range(1, planes)]
    peers += [(ctx, lax.rem(row + by, shards)) for by in range(1, shards)]
    for peer in peers:
        pl.semaphore_signal(barrier, inc=1, device_id=peer, device_id_type=MESH)
    if chain:
        near = jnp.where(ctx > 0, 1, 0) + jnp.where(ctx < last, 1, 0)
        pl.semaphore_wait(barrier, len(peers) + near)
    else:
        pl.semaphore_wait(barrier, len(peers))


class Job:
    def __init__(self, axis, rows, columns, first=0, share=0.5):
        self.axis, self.rows, self.columns, self.first = axis, rows, columns, first
        self.grain = 128 if axis else 16
        total = (columns if axis else rows) // self.grain
        assert total * self.grain == (columns if axis else rows)
        front = round(total * share)
        self.halves = front, total - front
        self.starts = 0, front
        self.half = front if front * CORES == total else None

    def span(self, start, size):
        start = start * self.grain
        if not isinstance(start, int):
            start = pl.multiple_of(start, self.grain)
        return pl.ds(start, size * self.grain)

    def cut(self, ref, start, size):
        span = self.span(start, size)
        return ref.at[:, span] if self.axis else ref.at[span, :]

    def index(self, start, size):
        span = self.span(start, size)
        return (slice(None), span) if self.axis else (span, slice(None))

    def shape(self, size):
        size = size * self.grain
        return (self.rows, size) if self.axis else (size, self.columns)

    def parts(self, planes, plane, core=0):
        base, extra = divmod(self.halves[core], planes)
        start = plane * base + jnp.minimum(plane, extra)
        found = []
        if base:
            found.append((start, base, None, 0))
        if extra:
            found.append((start + base, 1, plane < extra, base))
        return found

    def piece(self, planes):
        return -(-max(self.halves) // planes)


def flip(plane, bit):
    one = plane + 1 - 2 * lax.rem(plane, 2)
    if isinstance(bit, int):
        return one if bit == 1 else lax.rem(plane + 2, 4)
    return one * (2 - bit) + lax.rem(plane + 2, 4) * (bit - 1)


def guarded(cond, action):
    if cond is None:
        action()
    else:
        pl.when(cond)(action)


def remote(src, dst, send, recv, peer):
    return pltpu.make_async_remote_copy(
        src_ref=src, dst_ref=dst, send_sem=send, recv_sem=recv, device_id=peer,
        device_id_type=MESH,
    )


def best_job(rows, columns, share=0.5):
    return Job(0 if rows % 16 == 0 else 1, rows, columns, 0, share)


class Engine:
    def both(self, action, *given):
        def run():
            core = self.core

            def at(which):
                def branch():
                    self.core = which
                    action(*given)
                return branch

            pl.when(core == 0)(at(0))
            pl.when(core != 0)(at(1))
            self.core = core

        return run


class Gather(Engine):
    def __init__(self, jobs, arrays, owners=None):
        self.jobs, self.arrays = jobs, arrays
        self.owners = owners or list(range(len(jobs)))
        planes, shards = sizes()
        count = len(jobs)
        dma = pltpu.SemaphoreType.DMA
        self.outs = [jax.ShapeDtypeStruct((shards,) + a.shape, a.dtype) for a in arrays]
        self.scratch = [
            dma((count, shards, 2, 2)), dma((count, shards, max(planes, 5), 2, 2)),
            dma((count, shards, 2)), dma((len(arrays), 2)),
        ] + [pltpu.VMEM(a.shape, a.dtype) for a in arrays]
        self.units = [(j, by) for j in range(count) for by in range(1, shards)]

    def bind(self, srcs, dsts, sems):
        self.all_srcs, self.all_dsts = srcs, dsts
        self.srcs = [srcs[n] for n in self.owners]
        self.dsts = [dsts[n] for n in self.owners]
        self.sem_z, self.sem_p, self.sem_c, self.sem_l = sems[:4]
        self.staged = sems[4:]
        self.plane, self.core, self.row, self.planes, self.shards = place()

    def mine(self, j, plane=None):
        job = self.jobs[j]
        plane = self.plane if plane is None else plane
        for i, (start, size, cond, _) in enumerate(job.parts(self.planes, plane, self.core)):
            yield i, start + job.starts[self.core] + job.first, size, cond

    def fetch(self, n):
        return pltpu.make_async_copy(self.all_srcs[n], self.staged[n], self.sem_l.at[n, 0])

    def local(self, n):
        return pltpu.make_async_copy(
            self.staged[n], self.all_dsts[n].at[self.row], self.sem_l.at[n, 1]
        )

    def turn(self, by):
        return by + self.core * (self.shards - 2 * by)

    def origin(self, by):
        return lax.rem(self.row + self.shards - by, self.shards)

    def copy_z(self, j, by, i, start, size, incoming):
        job = self.jobs[j]
        sems = self.sem_z.at[j, by, i, 0], self.sem_z.at[j, by, i, 1]
        peer = (self.plane * CORES + self.core, lax.rem(self.row + by, self.shards))
        if incoming:
            ref = job.cut(self.dsts[j].at[self.origin(by)], start, size)
            return remote(ref, ref, *sems, peer)
        src = job.cut(self.srcs[j], start, size)
        return remote(src, job.cut(self.dsts[j].at[self.row], start, size), *sems, peer)

    def half(self, ref, job, part):
        if job.axis:
            cut = -(-job.rows // 32) * 16
            return ref.at[pl.ds(0, cut)] if part == 0 else ref.at[pl.ds(cut, job.rows - cut)]
        cut = -(-job.columns // 256) * 128
        if part == 0:
            return ref.at[:, pl.ds(0, cut)]
        return ref.at[:, pl.ds(cut, job.columns - cut)]

    def copy_p(self, j, by, q, i, start, size):
        job = self.jobs[j]
        sems = self.sem_p.at[j, by, q, i, 0], self.sem_p.at[j, by, q, i, 1]
        ref = job.cut(self.dsts[j].at[self.origin(by)], start, size)
        if self.planes != 4:
            peer = plane_peer(self.plane, self.core, self.row, self.planes, q)
            return remote(ref, ref, *sems, peer)
        if q > 2:
            ref, q = self.half(ref, job, q - 3), q - 2
        return remote(ref, ref, *sems, (flip(self.plane, q) * CORES + self.core, self.row))

    def copy_c(self, j, by, core):
        job = self.jobs[j]
        start = job.starts[core] + job.first
        ref = job.cut(self.dsts[j].at[self.origin(by)], start, job.halves[core])
        peer = (self.plane * CORES + 1 - self.core, self.row)
        return remote(ref, ref, self.sem_c.at[j, by, 0], self.sem_c.at[j, by, 1], peer)

    def open(self):
        for n in range(len(self.arrays)):
            self.fetch(n).start()

    def keep(self):
        for n in range(len(self.arrays)):
            self.fetch(n).wait()
            self.local(n).start()

    def start(self, j, by):
        by = self.turn(by)
        for i, start, size, cond in self.mine(j):
            guarded(cond, lambda: self.copy_z(j, by, i, start, size, False).start())

    def by_core(self, first, second):
        @pl.when(self.core == 0)
        def _():
            first()
            second()

        @pl.when(self.core != 0)
        def _():
            second()
            first()

    def spread(self, j, by):
        by = self.turn(by)
        for i, start, size, cond in self.mine(j):
            def forward():
                self.copy_z(j, by, i, start, size, True).wait_recv()
                if self.planes == 4:
                    self.by_core(
                        self.copy_p(j, by, 1, i, start, size).start,
                        lambda: self.copy_p(j, by, 2, i, start, size).start(),
                    )
                else:
                    for q in range(1, self.planes):
                        self.copy_p(j, by, q, i, start, size).start()
            guarded(cond, forward)

    def relay(self, j, by):
        if self.planes != 4:
            return
        by = self.turn(by)

        def one(bit):
            def run():
                for i, start, size, cond in self.mine(j, plane=flip(self.plane, bit)):
                    def pass_on():
                        self.copy_p(j, by, bit, i, start, size).wait_recv()
                        self.copy_p(j, by, 5 - bit, i, start, size).start()
                    guarded(cond, pass_on)
            return run

        self.by_core(one(2), one(1))

    def across(self, j, by):
        by = self.turn(by)
        if self.planes == 4:
            for i, start, size, cond in self.mine(j, plane=flip(flip(self.plane, 1), 2)):
                def both():
                    for q in (3, 4):
                        self.copy_p(j, by, q, i, start, size).wait_recv()
                guarded(cond, both)
        else:
            for q in range(1, self.planes):
                origin = lax.rem(self.plane + self.planes - q, self.planes)
                for i, start, size, cond in self.mine(j, plane=origin):
                    guarded(cond, lambda: self.copy_p(j, by, q, i, start, size).wait_recv())
        self.copy_c(j, by, self.core).start()

    def arrived(self, j):
        for by in range(1, self.shards):
            self.copy_c(j, by, 1 - self.core).wait_recv()

    def close(self):
        for j, by in self.units:
            self.copy_c(j, by, self.core).wait_send()
            for i, start, size, cond in self.mine(j):
                def sent():
                    self.copy_z(j, by, i, start, size, False).wait_send()
                    for q in (1, 2) if self.planes == 4 else range(1, self.planes):
                        self.copy_p(j, by, q, i, start, size).wait_send()
                guarded(cond, sent)
            if self.planes == 4:
                for bit in (1, 2):
                    for i, start, size, cond in self.mine(j, plane=flip(self.plane, bit)):
                        guarded(
                            cond,
                            lambda: self.copy_p(j, by, 5 - bit, i, start, size).wait_send(),
                        )
        self.settle()

    def settle(self):
        for n in range(len(self.arrays)):
            self.local(n).wait()


class GatherHere(Gather):
    def __init__(self, jobs, arrays, owners):
        super().__init__(jobs, arrays, owners)
        self.scratch = self.scratch[:4]

    def local(self, n):
        return pltpu.make_async_copy(
            self.all_srcs[n], self.all_dsts[n].at[self.row], self.sem_l.at[n, 1]
        )

    def open(self):
        for n in range(len(self.arrays)):
            self.local(n).start()

    def keep(self):
        pass

    def settle(self):
        pass


class Reduce(Engine):
    def __init__(self, jobs, arrays, keep=True, near=0):
        self.jobs, self.arrays, self.keep, self.near = jobs, arrays, keep, near
        planes, shards = sizes()
        count = len(jobs)
        dma = pltpu.SemaphoreType.DMA
        low = jnp.bfloat16
        refs = []
        for job in jobs:
            piece = job.piece(planes)
            refs += [
                pltpu.VMEM((shards,) + job.shape(max(job.halves)), low),
                pltpu.VMEM((shards,) + job.shape(max(job.halves)), low),
                pltpu.VMEM((shards, planes - 1) + job.shape(piece), low),
                pltpu.VMEM((shards,) + job.shape(piece), low),
                pltpu.VMEM((shards - 1,) + job.shape(piece), low),
            ]
        self.outs = [
            jax.ShapeDtypeStruct(job.shape(job.piece(planes)), low) for job in jobs if keep
        ]
        self.scratch = refs + [
            dma((count, shards, 3)), dma((count, shards, planes, 2, 2)),
            dma((count, shards, 2, 2)), dma((count,)),
        ]
        self.units = [(j, s) for s in range(shards) for j in range(count)]

    def bind(self, grads, outs, refs):
        count = len(self.jobs)
        self.grads, self.fins = grads, outs
        self.bufs = [refs[5 * j : 5 * j + 5] for j in range(count)]
        self.sem_a, self.sem_b, self.sem_c, self.sem_f = refs[5 * count :]
        self.plane, self.core, self.row, self.planes, self.shards = place()

    def owner(self, s):
        return lax.rem(self.row + 1 + s, self.shards)

    def sibling(self):
        return (self.plane * CORES + 1 - self.core, self.row)

    def locate(self, j, s):
        return self.grads[j].at[self.owner(s)]

    def copy_a(self, j, s, core):
        job = self.jobs[j]
        src = job.cut(self.locate(j, s), job.starts[core], job.halves[core])
        dst = job.cut(self.bufs[j][1].at[s], 0, job.halves[core])
        return remote(
            src, dst, self.sem_a.at[j, s, 0], self.sem_a.at[j, s, 1], self.sibling()
        )

    def load_a(self, j, s):
        job = self.jobs[j]
        src = job.cut(self.locate(j, s), job.starts[self.core], job.halves[self.core])
        dst = job.cut(self.bufs[j][0].at[s], 0, job.halves[self.core])
        return pltpu.make_async_copy(src, dst, self.sem_a.at[j, s, 2])

    def copy_b(self, j, s, slot, peer, i, start, size, at):
        job = self.jobs[j]
        src = job.cut(self.bufs[j][0].at[s], start, size)
        dst = job.cut(self.bufs[j][2].at[s, slot], at, size)
        sems = self.sem_b.at[j, s, slot, i, 0], self.sem_b.at[j, s, slot, i, 1]
        return remote(src, dst, *sems, (peer * CORES + self.core, self.row))

    def sends(self, j, s, second):
        if self.planes != 4:
            return [] if second else [
                (
                    q - 1, lax.rem(self.plane + q, self.planes),
                    lax.rem(self.plane + q, self.planes),
                )
                for q in range(1, self.planes)
            ]
        near, far = self.order(j, s)
        if second:
            return [(2, flip(self.plane, far), flip(self.plane, far))]
        peer = flip(self.plane, near)
        return [(0, peer, peer), (1, peer, flip(peer, far))]

    def order(self, j, s):
        near = 2 - self.core if self.near else 1 + (j + s + self.core) % 2
        return near, 3 - near

    def copy_c(self, j, s, i, size, at):
        job = self.jobs[j]
        src = job.cut(self.bufs[j][3].at[s], at, size)
        dst = job.cut(self.bufs[j][4].at[s], at, size)
        peer = (self.plane * CORES + self.core, self.owner(s))
        return remote(src, dst, self.sem_c.at[j, s, i, 0], self.sem_c.at[j, s, i, 1], peer)

    def parts(self, j, plane):
        return enumerate(self.jobs[j].parts(self.planes, plane, self.core))

    def a_start(self, j, s):
        self.copy_a(j, s, 1 - self.core).start()
        self.load_a(j, s).start()

    def b_start(self, j, s):
        own, came = self.bufs[j][0], self.bufs[j][1]
        self.load_a(j, s).wait()
        self.copy_a(j, s, self.core).wait_recv()
        at = (s,) + self.jobs[j].index(0, self.jobs[j].halves[self.core])
        own[at] = (own[at].astype(jnp.float32) + came[at].astype(jnp.float32)).astype(own.dtype)
        self.b_send(j, s, False)

    def b_send(self, j, s, second):
        for slot, peer, piece in self.sends(j, s, second):
            for i, (start, size, cond, at) in self.parts(j, piece):
                guarded(
                    cond, lambda: self.copy_b(j, s, slot, peer, i, start, size, at).start()
                )

    def b_next(self, j, s):
        if self.planes != 4:
            return
        job = self.jobs[j]
        own, came = self.bufs[j][0], self.bufs[j][2]
        near, far = self.order(j, s)
        for slot, piece in ((0, self.plane), (1, flip(self.plane, far))):
            for i, (start, size, cond, at) in self.parts(j, piece):
                def add():
                    self.copy_b(
                        j, s, slot, flip(self.plane, near), i, start, size, at
                    ).wait_recv()
                    at_own = (s,) + job.index(start, size)
                    got = came[(s, slot) + job.index(at, size)].astype(jnp.float32)
                    own[at_own] = (own[at_own].astype(jnp.float32) + got).astype(own.dtype)
                guarded(cond, add)
        self.b_send(j, s, True)

    def c_start(self, j, s):
        job = self.jobs[j]
        own, came, piece = self.bufs[j][0], self.bufs[j][2], self.bufs[j][3]
        slots = [2] if self.planes == 4 else range(self.planes - 1)
        for i, (start, size, cond, at) in self.parts(j, self.plane):
            def add():
                total = own[(s,) + job.index(start, size)].astype(jnp.float32)
                for slot in slots:
                    self.copy_b(j, s, slot, self.plane, i, start, size, at).wait_recv()
                    total = total + came[(s, slot) + job.index(at, size)].astype(jnp.float32)
                piece[(s,) + job.index(at, size)] = total.astype(piece.dtype)
                if s < self.shards - 1:
                    self.copy_c(j, s, i, size, at).start()
            guarded(cond, add)

    def total(self, j):
        job = self.jobs[j]
        piece, came = self.bufs[j][3], self.bufs[j][4]
        final = self.shards - 1
        for i, (start, size, cond, at) in self.parts(j, self.plane):
            def add():
                total = piece[(final,) + job.index(at, size)].astype(jnp.float32)
                for s in range(final):
                    self.copy_c(j, s, i, size, at).wait_recv()
                    total = total + came[(s,) + job.index(at, size)].astype(jnp.float32)
                piece[(final,) + job.index(at, size)] = total.astype(piece.dtype)
            guarded(cond, add)
        if self.keep:
            self.copy_f(j).start()

    def copy_f(self, j):
        return pltpu.make_async_copy(
            self.bufs[j][3].at[self.shards - 1], self.fins[j], self.sem_f.at[j]
        )

    def finish(self, j):
        if self.keep:
            self.copy_f(j).wait()
        for s in range(self.shards):
            self.copy_a(j, s, 1 - self.core).wait_send()
            for slot, peer, piece in self.sends(j, s, False) + self.sends(j, s, True):
                for i, (start, size, cond, at) in self.parts(j, piece):
                    guarded(
                        cond,
                        lambda: self.copy_b(j, s, slot, peer, i, start, size, at).wait_send(),
                    )
        for i, (start, size, cond, at) in self.parts(j, self.plane):
            def sent():
                for s in range(self.shards - 1):
                    self.copy_c(j, s, i, size, at).wait_send()
            guarded(cond, sent)


class ReduceHere(Reduce):
    def locate(self, j, s):
        return self.grads[j].at[s] if j == 0 else self.grads[j].at[self.owner(s)]


class Share(Engine):
    def __init__(self, jobs, arrays, source=None):
        self.jobs, self.arrays, self.source = jobs, arrays, source
        planes, _ = sizes()
        count = len(jobs)
        dma = pltpu.SemaphoreType.DMA
        self.outs = [
            jax.ShapeDtypeStruct((job.rows, job.columns), jnp.bfloat16) for job in jobs
        ]
        self.scratch = [dma((count, planes, 2, 2)), dma((count, 2))]
        if source is None:
            self.scratch += [pltpu.VMEM(a.shape, a.dtype) for a in arrays] + [dma((count,))]

    def bind(self, fins, outs, sems):
        if self.source is not None:
            fins = [bufs[3].at[self.source.shards - 1] for bufs in self.source.bufs]
        self.given = fins
        self.fins, self.outs_ref = fins, outs
        self.sem_d, self.sem_e = sems[:2]
        if self.source is None:
            self.fins, self.sem_f = sems[2:-1], sems[-1]
        self.plane, self.core, self.row, self.planes, self.shards = place()

    def parts(self, j, plane):
        return enumerate(self.jobs[j].parts(self.planes, plane, self.core))

    def fetch(self, j):
        return pltpu.make_async_copy(self.given[j], self.fins[j], self.sem_f.at[j])

    def copy_d(self, j, q, i, start, size, at):
        job = self.jobs[j]
        src = job.cut(self.fins[j], at, size)
        dst = job.cut(self.outs_ref[j], start + job.starts[self.core], size)
        sems = self.sem_d.at[j, q, i, 0], self.sem_d.at[j, q, i, 1]
        if q == 0:
            return pltpu.make_async_copy(src, dst, sems[0])
        return remote(
            src, dst, *sems, plane_peer(self.plane, self.core, self.row, self.planes, q)
        )

    def copy_e(self, j, core):
        job = self.jobs[j]
        ref = job.cut(self.outs_ref[j], job.starts[core], job.halves[core])
        peer = (self.plane * CORES + 1 - self.core, self.row)
        return remote(ref, ref, self.sem_e.at[j, 0], self.sem_e.at[j, 1], peer)

    def start(self, j):
        if self.source is None:
            self.fetch(j).wait()
        for i, (start, size, cond, at) in self.parts(j, self.plane):
            def send():
                for q in range(self.planes):
                    self.copy_d(j, q, i, start, size, at).start()
            guarded(cond, send)

    def across(self, j):
        for q in range(1, self.planes):
            origin = lax.rem(self.plane + self.planes - q, self.planes)
            for i, (start, size, cond, at) in self.parts(j, origin):
                guarded(cond, lambda: self.copy_d(j, q, i, start, size, at).wait_recv())
        for i, (start, size, cond, at) in self.parts(j, self.plane):
            guarded(cond, lambda: self.copy_d(j, 0, i, start, size, at).wait())
        self.copy_e(j, self.core).start()

    def finish(self, j):
        self.copy_e(j, 1 - self.core).wait_recv()
        self.copy_e(j, self.core).wait_send()
        for i, (start, size, cond, at) in self.parts(j, self.plane):
            def sent():
                for q in range(1, self.planes):
                    self.copy_d(j, q, i, start, size, at).wait_send()
            guarded(cond, sent)


def any_spec():
    return pl.BlockSpec(memory_space=pl.ANY)


def sizes():
    return lax.axis_size("ctx") // CORES, lax.axis_size("fsdp")


def fused_call(
    kernel, steps, args, in_specs, out_specs, out_shape, scratch, engines, schedule, end, ident,
    chain=False, cost=None,
):
    n_in, n_out, n_scr = len(args), len(out_shape), len(scratch)
    e_in = [len(e.arrays) for e in engines]
    e_out = [len(e.outs) for e in engines]
    e_scr = [len(e.scratch) for e in engines]

    def cut(refs, first, counts):
        groups = [refs[:first]]
        for count in counts:
            groups.append(refs[first : first + count])
            first += count
        return groups, refs[first:]

    def kern(*refs):
        ins, refs = cut(refs, n_in, e_in)
        outs, refs = cut(refs, n_out, e_out)
        scrs, refs = cut(refs, n_scr, e_scr)
        for k, engine in enumerate(engines):
            engine.bind(ins[k + 1], outs[k + 1], scrs[k + 1])
        step = pl.program_id(0)
        pl.when(step == 0)(lambda: greet(chain))
        for when in sorted(schedule):
            def act():
                for action in schedule[when]:
                    action()
            pl.when(step == when)(act)
        if kernel is not None:
            kernel(*ins[0], *outs[0], *scrs[0])
        def close():
            for action in end:
                action()
        pl.when(step == steps - 1)(close)

    flat = lambda groups: [item for group in groups for item in group]
    found = pl.pallas_call(
        kern,
        grid=(steps,),
        in_specs=list(in_specs) + [any_spec()] * sum(e_in),
        out_specs=list(out_specs) + [any_spec()] * sum(e_out),
        out_shape=list(out_shape) + flat([e.outs for e in engines]),
        scratch_shapes=list(scratch) + flat([e.scratch for e in engines]),
        compiler_params=pltpu.CompilerParams(
            vmem_limit_bytes=VMEM_BYTES, collective_id=ident, has_side_effects=True,
            fuse_transposed_lhs_in_matmul=True,
        ),
        cost_estimate=cost,
    )(*args, *flat([e.arrays for e in engines]))
    groups, _ = cut(found, n_out, e_out)
    return groups


def call(action, *given):
    return lambda: action(*given)


class HaloBack:
    def __init__(self, pairs, wide):
        self.arrays = []
        self.pairs = pairs
        dma = pltpu.SemaphoreType.DMA
        self.outs = [jax.ShapeDtypeStruct((2 * pairs, WINDOW, TILE), jnp.bfloat16)]
        self.scratch = [
            pltpu.VMEM((pairs, 2, WINDOW, TILE), jnp.bfloat16), dma((pairs, 2, 2)),
        ]

    def bind(self, _, outs, refs):
        (self.out,), (self.buf, self.sems) = outs, refs
        self.ctx, self.row = lax.axis_index("ctx"), lax.axis_index("fsdp")
        self.last = lax.axis_size("ctx") - 1

    def copy(self, pair, side):
        return remote(
            self.buf.at[pair, side], self.out.at[side * self.pairs + pair],
            self.sems.at[pair, side, 0], self.sems.at[pair, side, 1],
            (jnp.maximum(self.ctx - 1, 0), self.row),
        )

    def send(self, pair):
        @pl.when(self.ctx > 0)
        def _():
            for side in range(2):
                self.copy(pair, side).start()

    def finish(self):
        @pl.when(self.ctx > 0)
        def _():
            for pair in range(self.pairs):
                for side in range(2):
                    self.copy(pair, side).wait_send()

        @pl.when(self.ctx < self.last)
        def _():
            for pair in range(self.pairs):
                for side in range(2):
                    self.copy(pair, side).wait_recv()


class Small:
    def __init__(self, array):
        self.arrays = [array]
        planes, shards = sizes()
        dma = pltpu.SemaphoreType.DMA
        self.outs = [jax.ShapeDtypeStruct(array.shape, jnp.float32)]
        self.peers = 1, planes - 1, shards - 1
        self.scratch = [
            pltpu.VMEM((4,) + array.shape, jnp.float32),
            pltpu.VMEM((sum(self.peers),) + array.shape, jnp.float32),
            dma((sum(self.peers), 2)), dma((2,)),
        ]

    def bind(self, given, outs, refs):
        (self.given,), (self.out,) = given, outs
        self.own, self.came, self.sems, self.sem_l = refs
        self.plane, self.core, self.row, self.planes, self.shards = place()

    def load(self):
        return pltpu.make_async_copy(self.given, self.own.at[0], self.sem_l.at[0])

    def save(self):
        return pltpu.make_async_copy(self.own.at[3], self.out, self.sem_l.at[1])

    def copy(self, stage, n):
        at = sum(self.peers[:stage]) + n
        if stage == 0:
            peer = (self.plane * CORES + 1 - self.core, self.row)
        elif stage == 1:
            peer = plane_peer(self.plane, self.core, self.row, self.planes, n + 1)
        else:
            peer = (self.plane * CORES + self.core, lax.rem(self.row + n + 1, self.shards))
        return remote(
            self.own.at[stage], self.came.at[at], self.sems.at[at, 0], self.sems.at[at, 1], peer
        )

    def send(self, stage):
        for n in range(self.peers[stage]):
            self.copy(stage, n).start()

    def add(self, stage):
        total = self.own[stage]
        for n in range(self.peers[stage]):
            self.copy(stage, n).wait_recv()
            total = total + self.came[sum(self.peers[:stage]) + n]
        self.own[stage + 1] = total

    def finish(self):
        self.save().start()
        for stage in range(3):
            for n in range(self.peers[stage]):
                self.copy(stage, n).wait_send()
        self.save().wait()


def layer_norm(values, gain, shift):
    middle = jnp.mean(values, axis=-1, keepdims=True)
    centred = values - middle
    spread = jnp.mean(centred * centred, axis=-1, keepdims=True)
    return centred * lax.rsqrt(spread + epsilon) * gain + shift


def passed_along(value, axis, by):
    peers = lax.axis_size(axis)
    pairs = [(i, i + by) for i in range(peers) if 0 <= i + by < peers]
    return lax.ppermute(value, axis, pairs)


def segment_ids(lengths_row, positions):
    ends = jnp.cumsum(lengths_row)
    found = jnp.sum((positions[:, None] >= ends[None, :]).astype(jnp.int32), axis=1)
    return jnp.where(positions >= 0, found, -1)


def padded(array, parts):
    rows, columns = array.shape
    each = columns // parts
    wide = -(-each // TILE) * TILE
    array = array.reshape(rows, parts, each)
    return jnp.pad(array, ((0, 0), (0, 0), (0, wide - each))).reshape(rows, parts * wide)


def widened(array, columns):
    return jnp.pad(array, ((0, 0), (0, columns - array.shape[1])))


def even(columns):
    return -(-columns // (CORES * TILE)) * CORES * TILE


def on_device(
    activations, doc_lengths, cotangent, attn_gain, attn_shift, w_qkv, query_bias, value_bias,
    w_out, out_bias, mlp_gain, mlp_shift, w_fc, fc_bias, w_proj, proj_bias,
):
    low = jnp.bfloat16
    shards = lax.axis_size("fsdp")
    shard_rows, hidden = w_fc.shape
    features = activations.shape[2]
    wide = -(-features // TILE) * TILE
    pairs = wide // TILE
    qkv_wide, out_wide = even(3 * wide), even(features)
    own_hidden = w_proj.shape[0]
    first = own_hidden * 8 // 17
    second = own_hidden - first
    job_qkv, job_out = best_job(shard_rows, qkv_wide), best_job(shard_rows, out_wide)
    jobs_a = [best_job(shard_rows, shards * first), Job(0, first, features)]
    jobs_b = [best_job(shard_rows, shards * second), Job(0, second, features)]
    uneven_b = [
        best_job(shard_rows, shards * second, 0.35), Job(0, second, features, 0, 0.35)
    ]

    x_t, cot_t = activations[0].T, cotangent[0].T
    tok = x_t.shape[1]
    vectors = (
        attn_gain, attn_shift, query_bias, value_bias, out_bias, mlp_gain, mlp_shift, proj_bias,
    )
    vec = jnp.concatenate([v[None] for v in vectors] + [fc_bias.reshape(-1, shard_rows)])
    vec = jnp.pad(vec, ((0, 2 * TILE - vec.shape[0]), (0, 0))).T
    (
        qkv, halo, normed1_t, cot, vfull, qkv_w, fc_a, fc_b, proj_a, proj_b, out_low,
    ) = first_call(
        x_t, cot_t, w_qkv, vec, w_fc, w_proj, w_out, first, wide, qkv_wide, out_wide, 0
    )
    qkv_w = qkv_w.reshape(features, qkv_wide)
    vfull = vfull[:, :, :TILE].astype(jnp.float32)
    gain_one = vfull[:, :, 0].reshape(features, 1)
    vec_two = jnp.stack([vfull[:, :, n].reshape(-1) for n in (4, 5, 6, 7)])
    pbias = vec_two[3:4]
    fcbias = vfull[:, :, 8 : 8 + own_hidden // shard_rows].transpose(0, 2, 1)
    fcbias = fcbias.reshape(shards, own_hidden)

    first_pos = lax.axis_index("ctx") * tok
    ext_positions = first_pos - WINDOW + jnp.arange(tok + WINDOW, dtype=jnp.int32)
    doc_ext = segment_ids(doc_lengths[0], ext_positions)
    ids = jnp.arange(TILE, dtype=jnp.int32)[None, :]
    same = doc_ext[:, None] == ids
    qdoc = same[WINDOW:].astype(low)
    kdoc = jnp.where(same | (ids >= doc_lengths.shape[1]), 0.0, masked_score).astype(low)

    (attended, full, stat), (out_w, fc_wa, proj_wa) = attention_forward(
        qkv, halo, qdoc, kdoc, features,
        Gather([job_out] + jobs_a, [out_low, fc_a, proj_a]),
        1,
    )
    out_w = out_w.reshape(features, out_wide)
    lse = stat.T[: 2 * pairs].reshape(pairs, 2, tok)
    resid, normed2_low, normed2_t = out_norm(attended, out_w, x_t, vec_two)
    fcb_a = fcbias[:, :first].reshape(1, -1)
    fcb_b = fcbias[:, first:].reshape(1, -1)
    rest = Gather(jobs_b, [fc_b, proj_b])
    (base, dnorm_a, gproj_a, gfc_a, gfcb_a), (fc_wb, proj_wb) = mlp_part(
        normed2_low, normed2_t, cot, cot_t, resid, None, None,
        fc_wa.reshape(features, -1), fcb_a, proj_wa.reshape(-1, features),
        rest, *gather_plan(rest, shards * first // 256), 2,
    )
    sum_a = Reduce(
        jobs_a,
        [gfc_a.reshape(shards, shard_rows, -1), gproj_a.reshape(shards, first, features)],
    )
    schedule, end, done = reduce_plan(sum_a, shards * second // 256, shards * second // 256 - 3)
    (block_out, dnormed2, gproj_b, gfc_b, gfcb_b), fins_a = mlp_part(
        normed2_low, normed2_t, cot, cot_t, base, dnorm_a, pbias,
        fc_wb.reshape(features, -1), fcb_b, proj_wb.reshape(-1, features),
        sum_a, schedule, end + done, 3,
    )
    gresid_t, grad_attended, grad_wout, mid_sums = middle(
        dnormed2, resid, cot, attended, out_w, vec_two
    )
    sum_b = Reduce(
        uneven_b,
        [gfc_b.reshape(shards, shard_rows, -1), gproj_b.reshape(shards, second, features)],
        near=2,
    )
    (dq, dko, dvo), fins_b, (r_fca, r_proja), (back,) = attention_backward(
        qkv, halo, grad_attended, full, lse, qdoc, kdoc, features, sum_b,
        Share(jobs_a, fins_a), 4,
    )
    small = jnp.concatenate([
        jnp.zeros((4, features), jnp.float32),
        jnp.stack([mid_sums[2], mid_sums[0], mid_sums[1], mid_sums[3]]),
        jnp.concatenate(
            [gfcb_a.reshape(shards, first), gfcb_b.reshape(shards, second)], axis=1
        ).reshape(-1, features),
    ])
    small = jnp.pad(small, ((0, -small.shape[0] % 8), (0, 0)))
    input_grad_t, r_qkv, r_out, r_fcb, r_projb, small = last_call(
        [job_qkv, job_out], Share(uneven_b, fins_b), normed1_t, x_t, gain_one, dq, dko, dvo, back, qkv_w, gresid_t,
        grad_wout.reshape(shards, shard_rows, out_wide), small, 5,
    )
    r_qkv, r_out, r_fc, r_proj = finals(
        features, shards, r_qkv, r_out, r_fca, r_fcb, r_proja, r_projb
    )
    row = lax.axis_index("fsdp")
    sums = [
        lax.dynamic_slice_in_dim(small[n], row * shard_rows, shard_rows) for n in range(8)
    ]
    fcb_sum = lax.dynamic_slice_in_dim(
        small[8 : 8 + hidden // features].reshape(-1), row * own_hidden, own_hidden
    )
    return (
        block_out.T[None], input_grad_t.T[None], sums[0], sums[1], r_qkv, sums[2], sums[3], r_out,
        sums[4], sums[5], sums[6], r_fc, fcb_sum, r_proj, sums[7],
    )


def solution(mesh):
    vec, mat = P("fsdp"), P("fsdp", None)
    seq = P("fsdp", "ctx", None)
    placed = (
        seq, mat, seq, vec, vec, mat, vec, vec, mat, vec, vec, vec, mat, vec, mat, vec,
    )
    return jax.shard_map(
        on_device,
        mesh=mesh,
        in_specs=placed,
        out_specs=(seq, seq, vec, vec, mat, vec, vec, mat, vec, vec, vec, mat, vec, mat, vec),
        check_vma=False,
    )
```

```python
import math

import jax
import jax.numpy as jnp
from jax import lax
from jax.experimental import pallas as pl
from jax.experimental.pallas import tpu as pltpu
from jax.sharding import PartitionSpec as P

HEAD = 64
WINDOW = 1024
TILE = 128
ROWS = 256
LOG2E = 1.4426950408889634
epsilon = 1e-05
masked_score = -1e30
VMEM_BYTES = 60 * 1024 * 1024

NT = (((1,), (1,)), ((), ()))
TN = (((0,), (0,)), ((), ()))


def dot_f32(left, right, dims=(((1,), (0,)), ((), ()))):
    return lax.dot_general(left, right, dims, preferred_element_type=jnp.float32)


def head_lanes(rows, which):
    lane = lax.broadcasted_iota(jnp.int32, (rows, TILE), 1)
    return lane < HEAD if which == 0 else lane >= HEAD


def attention_forward_kernel(
    last, tok, q_ref, kh_ref, ko_ref, vh_ref, vo_ref, qdoc_ref, kdoc_ref,
    low_ref, full_ref, stat_ref, kcat, vcat,
):
    pair = pl.program_id(0)
    scale2 = LOG2E / math.sqrt(HEAD)
    span = ROWS + WINDOW

    @pl.when(pair == 0)
    def _():
        kcat[:, TILE:] = kdoc_ref[...]
        stat_ref[...] = jnp.zeros_like(stat_ref)

    kcat[:WINDOW, :TILE] = kh_ref[...]
    kcat[WINDOW:, :TILE] = ko_ref[...]
    vcat[:WINDOW] = vh_ref[...]
    vcat[WINDOW:] = vo_ref[...]
    row = lax.broadcasted_iota(jnp.int32, (ROWS, ROWS), 0)
    col = lax.broadcasted_iota(jnp.int32, (ROWS, ROWS), 1)
    lane = lax.broadcasted_iota(jnp.int32, (ROWS, TILE), 1)

    def one(block, which):
        rows = pl.ds(block * ROWS, ROWS)
        keys = pl.ds(block * ROWS, span)
        query = q_ref[rows, :]
        query = jnp.where(head_lanes(ROWS, which), query, jnp.zeros_like(query))
        query = jnp.concatenate([query, qdoc_ref[rows, :]], axis=1)
        scores = dot_f32(query, kcat[keys, :], NT)
        first = jnp.where(col >= row, scores[:, :ROWS], masked_score)
        final = jnp.where(col <= row, scores[:, WINDOW:], masked_score)
        scores = jnp.concatenate([first, scores[:, ROWS:WINDOW], final], axis=1)
        top = jnp.max(scores, axis=1, keepdims=True)
        expo = jnp.exp2((scores - top) * scale2)
        total = jnp.sum(expo, axis=1, keepdims=True)
        mixed = dot_f32(expo.astype(jnp.bfloat16), vcat[keys, :])
        stat = top * scale2 + jnp.log2(total)
        stat_ref[rows, :] = jnp.where(lane == 2 * pair + which, stat, stat_ref[rows, :])
        return mixed / total

    def block_out(heads):
        for block in range(tok // ROWS):
            rows = pl.ds(block * ROWS, ROWS)
            mixed = one(block, 0)
            other = one(block, 1) if heads == 2 else jnp.zeros_like(mixed)
            mixed = jnp.where(head_lanes(ROWS, 0), mixed, other)
            low_ref[rows, :] = mixed.astype(jnp.bfloat16)
            full_ref[rows, :] = mixed

    if last is None:
        block_out(2)
    else:
        pl.when(pair < last)(lambda: block_out(2))
        pl.when(pair == last)(lambda: block_out(1))


def attention_backward_kernel(
    last, tok, back, q_ref, kh_ref, ko_ref, vh_ref, vo_ref, do_ref, full_ref, lse_ref,
    qdoc_ref, kdoc_ref, dq_ref, dko_ref, dvo_ref,
    kcat, vcat, dk_acc, dv_acc, delta_ref,
):
    pair = pl.program_id(0)
    scale = 1.0 / math.sqrt(HEAD)
    scale2 = LOG2E * scale
    span = ROWS + WINDOW

    @pl.when(pair == 0)
    def _():
        kcat[:, TILE:] = kdoc_ref[...]

    kcat[:WINDOW, :TILE] = kh_ref[...]
    kcat[WINDOW:, :TILE] = ko_ref[...]
    vcat[:WINDOW] = vh_ref[...]
    vcat[WINDOW:] = vo_ref[...]
    dk_acc[...] = jnp.zeros_like(dk_acc)
    dv_acc[...] = jnp.zeros_like(dv_acc)
    key = lax.broadcasted_iota(jnp.int32, (ROWS, ROWS), 0)
    qry = lax.broadcasted_iota(jnp.int32, (ROWS, ROWS), 1)
    valid = head_lanes(tok, 0) | (pair < last if last is not None else True)
    product = jnp.where(valid, do_ref[...].astype(jnp.float32) * full_ref[...], 0.0)
    pick_row = lax.broadcasted_iota(jnp.int32, (8, TILE), 0)
    pick_lane = lax.broadcasted_iota(jnp.int32, (8, TILE), 1)
    pick = (pick_row == pick_lane // HEAD).astype(jnp.float32)
    delta_ref[...] = lax.dot_general(
        pick, product, NT, precision=lax.Precision.HIGHEST, preferred_element_type=jnp.float32
    )

    def one(block, which):
        rows = pl.ds(block * ROWS, ROWS)
        keys = pl.ds(block * ROWS, span)
        lanes = head_lanes(ROWS, which)
        query = q_ref[rows, :]
        query = jnp.where(lanes, query, jnp.zeros_like(query))
        upstream = do_ref[rows, :]
        upstream = jnp.where(lanes, upstream, jnp.zeros_like(upstream))
        query_doc = jnp.concatenate([query, qdoc_ref[rows, :]], axis=1)
        scores = dot_f32(kcat[keys, :], query_doc, NT)
        first = jnp.where(key >= qry, scores[:ROWS], masked_score)
        final = jnp.where(key <= qry, scores[WINDOW:], masked_score)
        scores = jnp.concatenate([first, scores[ROWS:WINDOW], final], axis=0)
        stat = lse_ref[0, which : which + 1, rows]
        delta = delta_ref[which : which + 1, rows]
        prob = jnp.exp2(scores * scale2 - stat)
        dprob = dot_f32(vcat[keys, :], upstream, NT)
        dscore = (prob * (dprob - delta)).astype(jnp.bfloat16)
        dv_acc[keys, :] += dot_f32(prob.astype(jnp.bfloat16), upstream)
        dk_acc[keys, :] += dot_f32(dscore, query)
        lanes_k = head_lanes(span, which)
        keys_one = kcat[keys, :TILE]
        keys_one = jnp.where(lanes_k, keys_one, jnp.zeros_like(keys_one))
        return dot_f32(dscore, keys_one, TN)

    def block_out(heads):
        for block in range(tok // ROWS):
            rows = pl.ds(block * ROWS, ROWS)
            dq = one(block, 0)
            if heads == 2:
                dq = dq + one(block, 1)
            dq_ref[rows, :] = (dq * scale).astype(jnp.bfloat16)

    if last is None:
        block_out(2)
    else:
        pl.when(pair < last)(lambda: block_out(2))
        pl.when(pair == last)(lambda: block_out(1))
    back.buf[pair, 0] = (dk_acc[:WINDOW] * scale).astype(jnp.bfloat16)
    back.buf[pair, 1] = dv_acc[:WINDOW].astype(jnp.bfloat16)
    back.send(pair)
    dko_ref[...] = (dk_acc[WINDOW:] * scale).astype(jnp.bfloat16)
    dvo_ref[...] = dv_acc[WINDOW:].astype(jnp.bfloat16)


def attention_forward(qkv, halo, qdoc, kdoc, features, engine, ident):
    tok = qkv.shape[0]
    pairs = -(-features // TILE)
    heads = features // HEAD
    last = pairs - 1 if heads % 2 else None
    blk = lambda off: pl.BlockSpec((tok, TILE), lambda p, off=off: (0, off + p))
    halo_blk = lambda off: pl.BlockSpec((WINDOW, TILE), lambda p, off=off: (0, off + p))
    fixed = lambda rows: pl.BlockSpec((rows, TILE), lambda p: (0, 0))
    return fused_call(
        lambda *refs: attention_forward_kernel(last, tok, *refs),
        pairs,
        (qkv, halo, qkv, halo, qkv, qdoc, kdoc),
        [
            blk(0), halo_blk(0), blk(pairs), halo_blk(pairs), blk(2 * pairs),
            fixed(tok), fixed(tok + WINDOW),
        ],
        [blk(0), blk(0), fixed(tok)],
        [
            jax.ShapeDtypeStruct((tok, features), jnp.bfloat16),
            jax.ShapeDtypeStruct((tok, pairs * TILE), jnp.float32),
            jax.ShapeDtypeStruct((tok, TILE), jnp.float32),
        ],
        [
            pltpu.VMEM((tok + WINDOW, 2 * TILE), jnp.bfloat16),
            pltpu.VMEM((tok + WINDOW, TILE), jnp.bfloat16),
        ],
        [engine],
        *gather_plan(engine, pairs),
        ident,
        cost=pl.CostEstimate(
            flops=4 * heads * tok * (ROWS + WINDOW) * HEAD * 4,
            bytes_accessed=tok * features * 20,
            transcendentals=heads * tok * (ROWS + WINDOW),
        ),
    )


def attention_backward(
    qkv, halo, upstream, full, lse, qdoc, kdoc, features, reduce, ident
):
    tok = qkv.shape[0]
    pairs = -(-features // TILE)
    heads = features // HEAD
    last = pairs - 1 if heads % 2 else None
    blk = lambda off: pl.BlockSpec((tok, TILE), lambda p, off=off: (0, off + p))
    halo_blk = lambda off: pl.BlockSpec((WINDOW, TILE), lambda p, off=off: (0, off + p))
    fixed = lambda rows: pl.BlockSpec((rows, TILE), lambda p: (0, 0))
    wide = pairs * TILE
    back = HaloBack(pairs, wide)
    schedule, end, done = reduce_plan(reduce, pairs, pairs - 3)
    end += done + [back.finish]
    return fused_call(
        lambda *refs: attention_backward_kernel(last, tok, back, *refs),
        pairs,
        (qkv, halo, qkv, halo, qkv, upstream, full, lse, qdoc, kdoc),
        [
            blk(0), halo_blk(0), blk(pairs), halo_blk(pairs), blk(2 * pairs),
            blk(0), blk(0), pl.BlockSpec((1, 2, tok), lambda p: (p, 0, 0)),
            fixed(tok), fixed(tok + WINDOW),
        ],
        [blk(0), blk(0), blk(0)],
        [
            jax.ShapeDtypeStruct((tok, wide), jnp.bfloat16),
            jax.ShapeDtypeStruct((tok, wide), jnp.bfloat16),
            jax.ShapeDtypeStruct((tok, wide), jnp.bfloat16),
        ],
        [
            pltpu.VMEM((tok + WINDOW, 2 * TILE), jnp.bfloat16),
            pltpu.VMEM((tok + WINDOW, TILE), jnp.bfloat16),
            pltpu.VMEM((tok + WINDOW, TILE), jnp.float32),
            pltpu.VMEM((tok + WINDOW, TILE), jnp.float32),
            pltpu.VMEM((8, tok), jnp.float32),
        ],
        [reduce, back],
        schedule,
        end,
        ident,
        chain=True,
        cost=pl.CostEstimate(
            flops=10 * heads * tok * (ROWS + WINDOW) * HEAD * 4,
            bytes_accessed=tok * features * 40,
            transcendentals=heads * tok * (ROWS + WINDOW),
        ),
    )


GELU_A = math.sqrt(2.0 / math.pi)
GELU_B = 0.044715


def mlp_kernel(
    steps, opening, norm_ref, normt_ref, cot_ref, cott_ref, base_ref, dbase_ref, pbias_ref, fc_ref, fcb_ref, proj_ref,
    out_ref, dnorm_ref, gproj_ref, gfc_ref, gfcb_ref, final_acc, act_s, dpre_s,
):
    step = pl.program_id(0)
    tok = norm_ref.shape[0]

    @pl.when(step == 0)
    def _():
        final_acc[...] = base_ref[...]
        dnorm_ref[...] = jnp.zeros_like(dnorm_ref) if opening else dbase_ref[...]

    bias_sum = jnp.zeros(gfcb_ref.shape, jnp.float32)
    for part in range(tok // ROWS):
        rows = pl.ds(part * ROWS, ROWS)
        pre = dot_f32(norm_ref[rows, :], fc_ref[...]) + fcb_ref[...]
        dact = dot_f32(cot_ref[rows, :], proj_ref[...], NT)
        square = pre * pre
        bent = jnp.tanh(GELU_A * pre * (1.0 + GELU_B * square))
        half = 0.5 * (1.0 + bent)
        act = (pre * half).astype(jnp.bfloat16)
        slope = half + 0.5 * pre * (1.0 - bent * bent) * (
            GELU_A * (1.0 + 3.0 * GELU_B * square)
        )
        dpre = (dact * slope).astype(jnp.bfloat16)
        act_s[rows, :] = act
        dpre_s[rows, :] = dpre
        bias_sum = bias_sum + jnp.sum(dpre.astype(jnp.float32), axis=0, keepdims=True)
        final_acc[rows, :] += dot_f32(act, proj_ref[...])
        dnorm_ref[rows, :] += dot_f32(dpre, fc_ref[...], NT)
    gfcb_ref[...] = bias_sum
    gproj_ref[...] = dot_f32(cott_ref[...], act_s[...]).T.astype(jnp.bfloat16)
    gfc_ref[...] = dot_f32(normt_ref[...], dpre_s[...]).astype(jnp.bfloat16)

    if not opening:

        @pl.when(step == steps - 1)
        def _():
            for at in range(0, tok, ROWS):
                done = final_acc[at : at + ROWS, :] + pbias_ref[...]
                out_ref[:, at : at + ROWS] = done.T.astype(jnp.bfloat16)


def mlp_part(
    norm, norm_t, cot, cot_t, base, dbase, pbias, fc_w, fcb, proj_w, engine, schedule, end, ident
):
    tok, features = cot.shape
    hidden = fc_w.shape[1]
    width = 256
    steps = hidden // width
    opening = dbase is None
    whole = lambda shape: pl.BlockSpec(shape, lambda j: (0, 0), pipeline_mode=pl.Buffered(1))
    cols = lambda rows: pl.BlockSpec((rows, width), lambda j: (0, j))
    rows = pl.BlockSpec((width, features), lambda j: (j, 0))
    struct = jax.ShapeDtypeStruct

    def kern(*refs):
        refs = list(refs)
        if not opening:
            mlp_kernel(steps, False, *refs)
            return
        att, w, xt, vec, cot_ref, cott_ref, fc, fcb_ref, proj = refs[:9]
        out, dnorm, gproj, gfc, gfcb, resid, norm_ref, normt_ref = refs[9:17]

        @pl.when(pl.program_id(0) == 0)
        def _():
            out_norm(att, w, xt, vec, resid, norm_ref, normt_ref)

        mlp_kernel(
            steps, True, norm_ref, normt_ref, cot_ref, cott_ref, resid, None, None, fc, fcb_ref,
            proj, out, dnorm, gproj, gfc, gfcb, out, *refs[17:]
        )

    if opening:
        attended, out_w, x_t, vec = norm
        args = (attended, out_w, x_t, vec, cot, cot_t, fc_w, fcb, proj_w)
    else:
        args = (norm, norm_t, cot, cot_t, base, dbase, pbias, fc_w, fcb, proj_w)
    extra = [] if opening else [pltpu.VMEM((tok, features), jnp.float32)]
    more = [
        struct((tok, features), jnp.float32), struct((tok, features), jnp.bfloat16),
        struct((features, tok), jnp.bfloat16),
    ] if opening else []
    return fused_call(
        kern,
        steps,
        args,
        [whole(a.shape) for a in args[:-3]] + [cols(features), cols(1), rows],
        [
            whole((tok, features) if opening else (features, tok)), whole((tok, features)), rows,
            cols(features), cols(1),
        ] + [whole(a.shape) for a in more],
        [
            struct((tok, features), jnp.float32)
            if opening else struct((features, tok), jnp.bfloat16),
            struct((tok, features), jnp.float32), struct((hidden, features), jnp.bfloat16),
            struct((features, hidden), jnp.bfloat16), struct((1, hidden), jnp.float32),
        ] + more,
        extra
        + [pltpu.VMEM((tok, width), jnp.bfloat16), pltpu.VMEM((tok, width), jnp.bfloat16)],
        [engine],
        schedule,
        end,
        ident,
        cost=pl.CostEstimate(
            flops=12 * tok * features * hidden,
            bytes_accessed=features * hidden * 8 + tok * features * 20,
            transcendentals=tok * hidden,
        ),
    )


def last_kernel(
    reduce, early, late, small, dims, normt_ref, xt_ref, gain_ref, dq_hbm, dk_hbm, dv_hbm, back_hbm, w_hbm,
    gresid_hbm, gout_hbm, fin_a, fin_b, small_hbm, out_hbm, rqkv_hbm, rout_hbm, ra_hbm, rb_hbm,
    small_out,
    g, back, w, resid, full, sums, column, sem_in, sem_out, *refs,
):
    features, tok, shards, wide = dims
    low = jnp.bfloat16
    own = []
    for engine in (reduce, early, late, small):
        own.append(refs[: len(engine.scratch)])
        refs = refs[len(engine.scratch) :]
    reduce.bind([full, gout_hbm], [], own[0])
    early.bind([fin_a, fin_b], [ra_hbm, rb_hbm], own[1])
    late.bind([], [rqkv_hbm, rout_hbm], own[2])
    small.bind([small_hbm], [small_out], own[3])
    ctx, last = lax.axis_index("ctx"), lax.axis_size("ctx") - 1
    loads = [
        pltpu.make_async_copy(src, dst, sem_in.at[n])
        for n, (src, dst) in enumerate((
            (dq_hbm, g.at[:, pl.ds(0, wide)]), (dk_hbm, g.at[:, pl.ds(wide, wide)]),
            (dv_hbm, g.at[:, pl.ds(2 * wide, wide)]), (back_hbm, back), (w_hbm, w),
            (gresid_hbm, resid),
        ))
    ]
    for item in loads:
        item.start()
    for j in (0, 1):
        early.fetch(j).start()
    small.load().start()
    sums[...] = jnp.zeros_like(sums)
    if g.shape[1] > 3 * wide:
        g[:, 3 * wide :] = jnp.zeros_like(g[:, 3 * wide :])
    greet()
    do = lambda action, *given: reduce.both(action, *given)()
    share = lambda engine, action, *given: engine.both(action, *given)()
    for s in range(shards):
        do(reduce.a_start, 1, s)
    for j in (0, 1):
        share(early, early.start, j)
    for item in loads[:4]:
        item.wait()

    @pl.when(ctx < last)
    def _():
        for at in range(0, tok, ROWS):
            some = slice(at, at + ROWS)
            for n in range(back.shape[0]):
                lanes = slice(wide + n * TILE, wide + (n + 1) * TILE)
                total = g[some, lanes].astype(jnp.float32) + back[n, some].astype(jnp.float32)
                g[some, lanes] = total.astype(low)

    def multiply(s):
        full[s] = dot_f32(normt_ref[reduce.owner(s)], g[...]).astype(low)
        do(reduce.a_start, 0, s)

    def columns():
        total = jnp.zeros((1, g.shape[1]), jnp.float32)
        for at in range(0, tok, ROWS):
            part = g[at : at + ROWS].astype(jnp.float32)
            total = total + jnp.sum(part, axis=0, keepdims=True)
        column[0:1] = total[:, :features]
        column[1:2] = total[:, 2 * wide : 2 * wide + features]

    def back_block(block):
        some = pl.ds(block * ROWS, ROWS)
        up = dot_f32(w[...], g[some, :], NT)
        x = xt_ref[:, some].astype(jnp.float32)
        centred = x - jnp.mean(x, axis=0, keepdims=True)
        inverse = lax.rsqrt(jnp.mean(centred * centred, axis=0, keepdims=True) + epsilon)
        hat = centred * inverse
        sums[:, 0:1] += jnp.sum(up * hat, axis=1, keepdims=True)
        sums[:, 1:2] += jnp.sum(up, axis=1, keepdims=True)
        up = up * gain_ref[...]
        lean = jnp.mean(up, axis=0, keepdims=True)
        tilt = jnp.mean(up * hat, axis=0, keepdims=True)
        resid[:, some] = resid[:, some] + inverse * (up - lean - hat * tilt)
        item = pltpu.make_async_copy(
            resid.at[:, some], out_hbm.at[:, some], sem_out.at[block]
        )
        item.start()
        return item

    multiply(0)
    for s in range(shards):
        do(reduce.b_start, 1, s)
    multiply(1)
    do(reduce.b_start, 0, 0)
    multiply(2)
    do(reduce.b_start, 0, 1)
    do(reduce.b_next, 1, 0)
    do(reduce.b_next, 1, 1)
    for s in range(3, shards):
        multiply(s)
    do(reduce.b_start, 0, 2)
    do(reduce.b_next, 0, 0)
    for s in range(2, shards):
        do(reduce.b_next, 1, s)
    for item in loads[4:]:
        item.wait()
    columns()
    for j in (0, 1):
        share(early, early.across, j)
    for s in range(3, shards):
        do(reduce.b_start, 0, s)
    saves = [back_block(0)]
    do(reduce.b_next, 0, 1)
    for s in range(shards):
        do(reduce.c_start, 1, s)
    saves.append(back_block(1))
    for s in range(2, shards):
        do(reduce.b_next, 0, s)
    do(reduce.c_start, 0, 0)
    saves.append(back_block(2))
    do(reduce.c_start, 0, 1)
    do(reduce.total, 1)
    share(late, late.start, 1)
    for block in range(3, tok // ROWS):
        saves.append(back_block(block))
    small.load().wait()
    small.own[0, 0:2] = sums[...].T[0:2]
    small.own[0, 2:4] = column[0:2]
    small.send(0)
    for s in range(2, shards):
        do(reduce.c_start, 0, s)
    small.add(0)
    small.send(1)
    do(reduce.total, 0)
    share(late, late.start, 0)
    small.add(1)
    small.send(2)
    share(late, late.across, 1)
    share(late, late.across, 0)
    small.add(2)
    small.finish()
    for j in (0, 1):
        share(early, early.finish, j)
        share(late, late.finish, j)
        do(reduce.finish, j)
    for item in saves:
        item.wait()


def last_call(
    jobs, early, normt, x_t, gain, dq, dk, dv, back, weights, gresid_t, gout, small, ident
):
    features, tok = x_t.shape
    shards = sizes()[1]
    wide, qkv_wide = dq.shape[1], weights.shape[1]
    low, struct = jnp.bfloat16, jax.ShapeDtypeStruct
    rows = features // shards
    reduce = ReduceHere(jobs, [struct((shards, rows, qkv_wide), low), gout], keep=False)
    late, tiny = Share(jobs, [], reduce), Small(small)
    vm = pl.BlockSpec(memory_space=pltpu.VMEM)
    dma = pltpu.SemaphoreType.DMA
    return pl.pallas_call(
        lambda *refs: last_kernel(
            reduce, early, late, tiny, (features, tok, shards, wide), *refs
        ),
        in_specs=[vm] * 3 + [any_spec()] * 10,
        out_specs=[any_spec()] * 6,
        out_shape=[struct((features, tok), jnp.float32)] + late.outs + early.outs + tiny.outs,
        scratch_shapes=[
            pltpu.VMEM((tok, qkv_wide), low), pltpu.VMEM(back.shape, low),
            pltpu.VMEM((features, qkv_wide), low), pltpu.VMEM((features, tok), jnp.float32),
            pltpu.VMEM((shards, rows, qkv_wide), low), pltpu.VMEM((features, TILE), jnp.float32),
            pltpu.VMEM((8, features), jnp.float32), dma((6,)), dma((tok // ROWS,)),
        ] + reduce.scratch + early.scratch + late.scratch + tiny.scratch,
        compiler_params=pltpu.CompilerParams(
            vmem_limit_bytes=VMEM_BYTES, collective_id=ident, has_side_effects=True
        ),
    )(
        normt.reshape(shards, rows, tok), x_t, gain, dq, dk, dv, back, weights, gresid_t, gout,
        *early.arrays, small,
    )


def at_step(schedule, end, steps, when, action):
    if when < steps:
        schedule.setdefault(when, []).append(action)
    else:
        end.append(action)


def gather_plan(engine, steps, deep=3):
    schedule, end = {0: [engine.open]}, []
    units = engine.units
    for unit in units[:deep]:
        schedule[0].append(engine.both(engine.start, *unit))
    count = len(units)
    late = []
    at_step(schedule, end, steps, 1, engine.keep)
    for n, unit in enumerate(units):
        when = 2 + n * (steps - 4) // count
        at_step(schedule, end, steps, when, engine.both(engine.spread, *unit))
        if n + deep < count:
            at_step(schedule, end, steps, when, engine.both(engine.start, *units[n + deep]))
        late.append((when + 1, engine.both(engine.relay, *unit)))
    for when, action in late:
        at_step(schedule, end, steps, when, action)
    for (when, _), unit in zip(late, units):
        at_step(schedule, end, steps, when + 1, engine.both(engine.across, *unit))
    end += [engine.both(engine.arrived, j) for j in range(len(engine.jobs))]
    end.append(engine.both(engine.close))
    return schedule, end


def reduce_plan(engine, steps, span):
    schedule, end = {}, []
    units = engine.units
    late, later = [], []
    for n, unit in enumerate(units):
        when = n * span // len(units)
        at_step(schedule, end, steps, when, engine.both(engine.a_start, *unit))
        late.append((when + 1, engine.both(engine.b_start, *unit)))
    for when, action in late:
        at_step(schedule, end, steps, when, action)
    for n, unit in enumerate(units):
        at_step(schedule, end, steps, n * span // len(units) + 2, engine.both(engine.b_next, *unit))
    for n, unit in enumerate(units):
        at_step(schedule, end, steps, n * span // len(units) + 3, engine.both(engine.c_start, *unit))
    jobs = range(len(engine.jobs))
    end += [engine.both(engine.total, j) for j in jobs]
    return schedule, end, [engine.both(engine.finish, j) for j in jobs]


def joined(ref, cols):
    shards, rows, _ = ref.shape
    value = ref[:, :, cols]
    if rows % 16:
        value = value.astype(jnp.float32)
    return value.reshape(shards * rows, value.shape[2]).astype(jnp.bfloat16)


def first_kernel(
    engine, dims, xt_ref, ct_ref, wqkv_ref, vec_ref, fc_hbm, proj_hbm, out_hbm,
    qkv_hbm, halo_hbm, normt_hbm, cot_hbm, vfull_ref, wfull_hbm, fca_hbm, fcb_hbm, pa_hbm, pb_hbm,
    outl_hbm, qkv_ref, halo_ref, normt_ref, cot_ref,
    wsrc, vsrc, xh, norm, normh, bias, fc32, proj32, out32, fca_s, fcb_s, pa_s, pb_s, outl_s,
    sem_in, sem_out, sem_x, sem_done, *sems,
):
    features, tok, shards, first, wide, chunk = dims
    low = jnp.bfloat16
    rows = wqkv_ref.shape[0]
    own = proj_hbm.shape[0]
    second = own - first
    parts = (wsrc.shape[1] + chunk - 1) // chunk
    wsrcs, ws, sems = sems[:parts], sems[parts : 2 * parts], sems[2 * parts :]
    engine.bind([vsrc] + list(wsrcs), [vfull_ref] + list(ws), sems)
    ctx, row, last = lax.axis_index("ctx"), lax.axis_index("fsdp"), lax.axis_size("ctx") - 1

    def load(n, src, dst):
        return pltpu.make_async_copy(src, dst, sem_in.at[n])

    cut = fc32.shape[0]
    deep = proj32.shape[0]
    loads = [
        load(0, fc_hbm.at[pl.ds(0, cut)], fc32), load(1, proj_hbm.at[pl.ds(0, deep)], proj32),
        load(2, out_hbm, out32),
    ]
    for item in loads:
        item.start()
    wsrc[...] = jnp.zeros_like(wsrc)
    for n in range(3):
        wsrc[:, n * wide : n * wide + features] = wqkv_ref[
            :, n * features : (n + 1) * features
        ].astype(low)
    vsrc[...] = vec_ref[...].astype(low)
    for n in range(parts):
        wsrcs[n][...] = wsrc[:, n * chunk : min((n + 1) * chunk, wsrc.shape[1])]
    greet(True)
    halo_copy = remote(
        xt_ref, xh, sem_x.at[0], sem_x.at[1], (jnp.minimum(ctx + 1, last), row)
    )
    units = engine.units
    engine.open()
    for unit in units[: shards - 1]:
        engine.both(engine.start, *unit)()
    done = []

    def ready(n, src, dst):
        item = pltpu.make_async_copy(src, dst, sem_done.at[n])
        item.start()
        done.append(item)

    @pl.when(ctx == 0)
    def _():
        xh[...] = jnp.zeros_like(xh)

    saves = [
        pltpu.make_async_copy(src, dst, sem_out.at[n])
        for n, (src, dst) in enumerate(
            ((fca_s, fca_hbm), (fcb_s, fcb_hbm), (pa_s, pa_hbm), (pb_s, pb_hbm),
             (outl_s, outl_hbm))
        )
    ]

    def cast_fc(at):
        load(0, fc_hbm.at[pl.ds(at, cut)], fc32).wait()
        for n in range(shards):
            fca_s[at : at + cut, n * first : (n + 1) * first] = fc32[
                :, n * own : n * own + first
            ].astype(low)
            fcb_s[at : at + cut, n * second : (n + 1) * second] = fc32[
                :, n * own + first : (n + 1) * own
            ].astype(low)
        if at + cut < rows:
            load(0, fc_hbm.at[pl.ds(at + cut, cut)], fc32).start()

    def cast_proj(at):
        load(1, proj_hbm.at[pl.ds(at, deep)], proj32).wait()
        stop = min(max(first - at, 0), deep)
        if stop:
            pa_s[at : at + stop] = proj32[:stop].astype(low)
        if stop < deep:
            pb_s[at + stop - first : at + deep - first] = proj32[stop:].astype(low)
        if at + deep < own:
            load(1, proj_hbm.at[pl.ds(at + deep, deep)], proj32).start()

    def cast_out():
        load(2, out_hbm, out32).wait()
        outl_s[...] = jnp.zeros_like(outl_s)
        outl_s[:, :features] = out32[...].astype(low)
        for item in saves:
            item.start()

    def turn_cot():
        for at in range(0, tok, ROWS):
            cot_ref[at : at + ROWS, :] = ct_ref[:, at : at + ROWS].T
        ready(3, cot_ref, cot_hbm)

    def vectors():
        engine.both(engine.arrived, 0)()
        engine.local(0).wait()
        columns = vfull_ref[...].astype(jnp.float32).reshape(features, vfull_ref.shape[2])
        columns = columns[:, :TILE]
        lines = columns.T
        bias[...] = jnp.zeros_like(bias)
        bias[0:1, :features] = lines[2:3]
        bias[0:1, 2 * wide : 2 * wide + features] = lines[3:4]
        return columns

    def normalise(src, columns, dst, dst_t):
        gain, shift = columns[:, 0:1], columns[:, 1:2]
        for at in range(0, tok, ROWS):
            x = src[:, at : at + ROWS].astype(jnp.float32)
            centred = x - jnp.mean(x, axis=0, keepdims=True)
            spread = jnp.mean(centred * centred, axis=0, keepdims=True)
            y = centred * lax.rsqrt(spread + epsilon) * gain + shift
            if dst_t is not None:
                dst_t[:, at : at + ROWS] = y.astype(low)
            dst[at : at + ROWS, :] = y.T.astype(low)

    def multiply(n):
        engine.both(engine.arrived, 1 + n)()
        engine.local(1 + n).wait()
        lo, hi = n * chunk, min((n + 1) * chunk, wsrc.shape[1])
        weights = joined(ws[n], slice(0, hi - lo))
        item = pltpu.make_async_copy(
            ws[n], wfull_hbm.at[:, :, pl.ds(lo, hi - lo)], sem_done.at[12 + n]
        )
        item.start()
        done.append(item)
        for at in range(0, tok, ROWS):
            part = dot_f32(norm[at : at + ROWS, :], weights) + bias[0:1, lo:hi]
            qkv_ref[at : at + ROWS, lo:hi] = part.astype(low)
        ready(4 + 2 * n, qkv_ref.at[:, pl.ds(lo, hi - lo)], qkv_hbm.at[:, pl.ds(lo, hi - lo)])
        lo_h, hi_h = max(lo, wide), min(hi, 3 * wide)
        if lo_h >= hi_h:
            return
        weights = weights[:, lo_h - lo : hi_h - lo]
        for at in range(0, tok, ROWS):
            part = dot_f32(normh[at : at + ROWS, :], weights) + bias[0:1, lo_h:hi_h]
            halo_ref[at : at + ROWS, lo_h - wide : hi_h - wide] = part.astype(low)
        span = pl.ds(lo_h - wide, hi_h - lo_h)
        ready(5 + 2 * n, halo_ref.at[:, span], halo_hbm.at[:, span])

    per = shards - 1
    groups = [units[n : n + per] for n in range(0, len(units), per)]
    chunks = groups[1:]

    def each(action, group):
        for unit in group:
            engine.both(action, *unit)()

    for group in chunks[:2]:
        each(engine.start, group)
    pl.when(ctx < last)(lambda: halo_copy.start())
    for at in range(0, rows, cut):
        cast_fc(at)
    each(engine.spread, groups[0])
    each(engine.spread, chunks[0])
    for at in range(0, own, deep):
        cast_proj(at)
    cast_out()
    each(engine.relay, groups[0])
    each(engine.relay, chunks[0])
    each(engine.spread, chunks[1])
    each(engine.start, chunks[2])
    turn_cot()
    each(engine.across, groups[0])
    each(engine.across, chunks[0])
    each(engine.relay, chunks[1])
    each(engine.start, chunks[3])
    columns = vectors()
    normalise(xt_ref, columns, norm, normt_ref)
    ready(2, normt_ref, normt_hbm)
    each(engine.spread, chunks[2])
    each(engine.across, chunks[1])
    multiply(0)
    each(engine.spread, chunks[3])
    each(engine.relay, chunks[2])

    @pl.when(ctx > 0)
    def _():
        halo_copy.wait_recv()

    normalise(xh, columns, normh, None)
    each(engine.relay, chunks[3])
    each(engine.across, chunks[2])
    multiply(1)
    each(engine.across, chunks[3])
    multiply(2)
    multiply(3)
    engine.both(engine.close)()
    pl.when(ctx < last)(lambda: halo_copy.wait_send())
    for item in saves + done:
        item.wait()


def first_call(xt, ct, w_qkv, vec, w_fc, w_proj, w_out, first, wide, qkv_wide, out_wide, ident):
    features, tok = xt.shape
    planes, shards = sizes()
    rows, own = w_qkv.shape[0], w_proj.shape[0]
    low = jnp.bfloat16
    chunk = CORES * 4 * TILE
    columns = vec.shape[1]
    struct = jax.ShapeDtypeStruct
    wides = [columns] + [min(chunk, qkv_wide - at) for at in range(0, qkv_wide, chunk)]
    jobs = [best_job(rows, n) for n in wides]
    engine = GatherHere(jobs, [struct((rows, n), low) for n in wides], list(range(len(jobs))))
    dims = features, tok, shards, first, wide, chunk
    vm = pl.BlockSpec(memory_space=pltpu.VMEM)
    second = own - first
    cut = rows // 2 if rows // 2 % 8 == 0 else rows
    dma = pltpu.SemaphoreType.DMA
    return pl.pallas_call(
        lambda *refs: first_kernel(engine, dims, *refs),
        in_specs=[vm] * 4 + [any_spec()] * 3,
        out_specs=[any_spec()] * 4 + [vm] + [any_spec()] * 6,
        out_shape=[
            struct((tok, qkv_wide), low), struct((tok, 2 * wide), low), struct((features, tok), low),
            struct((tok, features), low), struct((shards, rows, columns), low),
            struct((shards, rows, qkv_wide), low), struct((rows, shards * first), low),
            struct((rows, shards * second), low), struct((first, features), low),
            struct((second, features), low), struct((rows, out_wide), low),
        ],
        scratch_shapes=[
            pltpu.VMEM((tok, qkv_wide), low), pltpu.VMEM((tok, 2 * wide), low),
            pltpu.VMEM((features, tok), low), pltpu.VMEM((tok, features), low),
            pltpu.VMEM((rows, qkv_wide), low),
            pltpu.VMEM((rows, columns), low), pltpu.VMEM((features, tok), low),
            pltpu.VMEM((tok, features), low), pltpu.VMEM((tok, features), low),
            pltpu.VMEM((8, qkv_wide), jnp.float32), pltpu.VMEM((cut, w_fc.shape[1]), jnp.float32),
            pltpu.VMEM((own // 2, features), jnp.float32),
            pltpu.VMEM((rows, features), jnp.float32),
            pltpu.VMEM((rows, shards * first), low), pltpu.VMEM((rows, shards * second), low),
            pltpu.VMEM((first, features), low), pltpu.VMEM((second, features), low),
            pltpu.VMEM((rows, out_wide), low), dma((3,)), dma((6,)), dma((2,)),
            dma((16,)),
        ] + [pltpu.VMEM((rows, n), low) for n in wides[1:]]
        + [pltpu.VMEM((shards, rows, n), low) for n in wides[1:]] + engine.scratch,
        compiler_params=pltpu.CompilerParams(
            vmem_limit_bytes=VMEM_BYTES, collective_id=ident, has_side_effects=True
        ),
    )(xt, ct, w_qkv, vec, w_fc, w_proj, w_out)


def final_kernel(
    features, shards, qkv_ref, out_ref, fca_ref, fcb_ref, block_ref, input_ref, pa_ref, pb_ref,
    gqkv_ref, gout_ref, gfc_ref, block_out, input_out, gproj_ref,
):
    step = pl.program_id(0)
    block_out[...] = block_ref[...]
    input_out[...] = input_ref[...]
    wide = -(-features // TILE) * TILE
    for n in range(3):
        gqkv_ref[:, n * features : (n + 1) * features] = qkv_ref[
            :, n * wide : n * wide + features
        ].astype(jnp.float32)
    gout_ref[...] = out_ref[:, :features].astype(jnp.float32)
    own, first = gfc_ref.shape[1] // shards, fca_ref.shape[1] // shards
    second = own - first
    for n in range(shards):
        gfc_ref[:, n * own : n * own + first] = fca_ref[
            :, n * first : (n + 1) * first
        ].astype(jnp.float32)
        gfc_ref[:, n * own + first : (n + 1) * own] = fcb_ref[
            :, n * second : (n + 1) * second
        ].astype(jnp.float32)
    rows = gproj_ref.shape[0]

    def proj(at):
        stop = min(max(first - at * rows, 0), rows)
        if stop:
            gproj_ref[:stop] = pa_ref[at * rows : at * rows + stop].astype(jnp.float32)
        if stop < rows:
            low = at * rows + stop - first
            gproj_ref[stop:] = pb_ref[low : low + rows - stop].astype(jnp.float32)

    for at in range(own // rows):
        pl.when(step == at)(call(proj, at))


def finals(
    features, shards, r_qkv, r_out, r_fca, r_fcb, block_out, input_grad, r_proja, r_projb
):
    rows, own = r_qkv.shape[0], r_proja.shape[0] + r_projb.shape[0]
    steps = 2 if rows // 2 % 8 == 0 else 1
    blk = lambda a: pl.BlockSpec((a.shape[0] // steps, a.shape[1]), lambda i: (i, 0))
    whole = lambda a: pl.BlockSpec(a.shape, lambda i: (0, 0), pipeline_mode=pl.Buffered(1))
    struct = jax.ShapeDtypeStruct
    shapes = [(rows, 3 * features), (rows, features), (rows, own * shards), (own, features)]
    shapes = [struct(s, jnp.float32) for s in shapes]
    shapes[3:3] = [struct(a.shape, a.dtype) for a in (block_out, input_grad)]
    return pl.pallas_call(
        lambda *refs: final_kernel(features, shards, *refs),
        grid=(steps,),
        in_specs=[blk(a) for a in (r_qkv, r_out, r_fca, r_fcb, block_out, input_grad)]
        + [whole(r_proja), whole(r_projb)],
        out_specs=[blk(s) for s in shapes],
        out_shape=shapes,
        compiler_params=pltpu.CompilerParams(vmem_limit_bytes=VMEM_BYTES),
    )(r_qkv, r_out, r_fca, r_fcb, block_out, input_grad, r_proja, r_projb)


def out_norm(att_ref, w_ref, xt_ref, vec_ref, resid_ref, norm_ref, normt_ref):
    tok, features = resid_ref.shape
    for at in range(0, tok, ROWS):
        rows = pl.ds(at, ROWS)
        mixed = dot_f32(att_ref[rows, :], w_ref[...])[:, :features] + vec_ref[0:1]
        resid = xt_ref[:, rows].astype(jnp.float32).T + mixed
        resid_ref[rows, :] = resid
        centred = resid - jnp.mean(resid, axis=1, keepdims=True)
        spread = jnp.mean(centred * centred, axis=1, keepdims=True)
        normed = centred * lax.rsqrt(spread + epsilon) * vec_ref[1:2] + vec_ref[2:3]
        norm_ref[rows, :] = normed.astype(jnp.bfloat16)
        normt_ref[:, rows] = normed.T.astype(jnp.bfloat16)


def middle_kernel(
    steps, dnorm_ref, resid_ref, cot_ref, att_ref, w_ref, vec_ref,
    gresid_ref, datt_ref, gout_ref, sums_ref, branch_t,
):
    step = pl.program_id(0)
    features = resid_ref.shape[1]

    @pl.when(step == 0)
    def _():
        sums_ref[...] = jnp.zeros_like(sums_ref)

    up, resid = dnorm_ref[...], resid_ref[...]
    cot = cot_ref[...].astype(jnp.float32)
    centred = resid - jnp.mean(resid, axis=1, keepdims=True)
    inverse = lax.rsqrt(jnp.mean(centred * centred, axis=1, keepdims=True) + epsilon)
    hat = centred * inverse
    sums_ref[0:1] += jnp.sum(up * hat, axis=0, keepdims=True)
    sums_ref[1:2] += jnp.sum(up, axis=0, keepdims=True)
    sums_ref[3:4] += jnp.sum(cot, axis=0, keepdims=True)
    up = up * vec_ref[1:2]
    lean = jnp.mean(up, axis=1, keepdims=True)
    tilt = jnp.mean(up * hat, axis=1, keepdims=True)
    gresid = cot + inverse * (up - lean - hat * tilt)
    turned = gresid.T
    gresid_ref[...] = turned
    branch = gresid.astype(jnp.bfloat16)
    branch_t[:, pl.ds(pl.multiple_of(step * ROWS, ROWS), ROWS)] = turned.astype(jnp.bfloat16)
    sums_ref[2:3] += jnp.sum(branch.astype(jnp.float32), axis=0, keepdims=True)
    datt_ref[...] = dot_f32(branch, w_ref[:, :features], NT).astype(jnp.bfloat16)

    @pl.when(step == steps - 1)
    def _():
        gout_ref[:, features:] = jnp.zeros_like(gout_ref[:, features:])
        for at in range(0, features, ROWS):
            some = slice(at, min(at + ROWS, features))
            grad = dot_f32(branch_t[some, :], att_ref[...])
            gout_ref[:, some] = grad.T.astype(jnp.bfloat16)


def middle(dnorm, resid, cot, attended, out_w, vec, share, ident):
    tok, features = resid.shape
    steps = tok // ROWS
    blk = pl.BlockSpec((ROWS, features), lambda i: (i, 0))
    blk_t = pl.BlockSpec((features, ROWS), lambda i: (0, i))
    whole = lambda shape: pl.BlockSpec(shape, lambda i: (0, 0), pipeline_mode=pl.Buffered(1))
    struct = jax.ShapeDtypeStruct
    those = range(len(share.jobs))
    schedule = {
        0: [call(lambda j: share.fetch(j).start(), j) for j in those],
        1: [share.both(share.start, j) for j in those],
        3: [share.both(share.across, j) for j in those],
    }
    return fused_call(
        lambda *refs: middle_kernel(steps, *refs),
        steps,
        (dnorm, resid, cot, attended, out_w, vec),
        [blk, blk, blk, whole(attended.shape), whole(out_w.shape), whole(vec.shape)],
        [blk_t, blk, whole(out_w.shape), whole((8, features))],
        [
            struct((features, tok), jnp.float32), struct((tok, features), jnp.bfloat16),
            struct(out_w.shape, jnp.bfloat16), struct((8, features), jnp.float32),
        ],
        [pltpu.VMEM((features, tok), jnp.bfloat16)],
        [share],
        schedule,
        [share.both(share.finish, j) for j in those],
        ident,
    )


MESH = pl.DeviceIdType.MESH
CORES = 2


def place():
    ctx, row = lax.axis_index("ctx"), lax.axis_index("fsdp")
    planes, shards = lax.axis_size("ctx") // CORES, lax.axis_size("fsdp")
    return ctx // CORES, lax.rem(ctx, CORES), row, planes, shards


def plane_peer(plane, core, row, planes, by):
    return (lax.rem(plane + by, planes) * CORES + core, row)


def greet(chain=False):
    plane, core, row, planes, shards = place()
    ctx = plane * CORES + core
    barrier = pltpu.get_barrier_semaphore()
    if chain:
        last = planes * CORES - 1

        @pl.when(ctx > 0)
        def _():
            pl.semaphore_signal(barrier, inc=1, device_id=(ctx - 1, row), device_id_type=MESH)

        @pl.when(ctx < last)
        def _():
            pl.semaphore_signal(barrier, inc=1, device_id=(ctx + 1, row), device_id_type=MESH)

    peers = [(plane * CORES + 1 - core, row)]
    peers += [plane_peer(plane, core, row, planes, by) for by in range(1, planes)]
    peers += [(ctx, lax.rem(row + by, shards)) for by in range(1, shards)]
    for peer in peers:
        pl.semaphore_signal(barrier, inc=1, device_id=peer, device_id_type=MESH)
    if chain:
        near = jnp.where(ctx > 0, 1, 0) + jnp.where(ctx < last, 1, 0)
        pl.semaphore_wait(barrier, len(peers) + near)
    else:
        pl.semaphore_wait(barrier, len(peers))


class Job:
    def __init__(self, axis, rows, columns, first=0, share=0.5):
        self.axis, self.rows, self.columns, self.first = axis, rows, columns, first
        self.grain = 128 if axis else 16
        total = (columns if axis else rows) // self.grain
        assert total * self.grain == (columns if axis else rows)
        front = round(total * share)
        self.halves = front, total - front
        self.starts = 0, front
        self.half = front if front * CORES == total else None

    def span(self, start, size):
        start = start * self.grain
        if not isinstance(start, int):
            start = pl.multiple_of(start, self.grain)
        return pl.ds(start, size * self.grain)

    def cut(self, ref, start, size):
        span = self.span(start, size)
        return ref.at[:, span] if self.axis else ref.at[span, :]

    def index(self, start, size):
        span = self.span(start, size)
        return (slice(None), span) if self.axis else (span, slice(None))

    def shape(self, size):
        size = size * self.grain
        return (self.rows, size) if self.axis else (size, self.columns)

    def parts(self, planes, plane, core=0):
        base, extra = divmod(self.halves[core], planes)
        start = plane * base + jnp.minimum(plane, extra)
        found = []
        if base:
            found.append((start, base, None, 0))
        if extra:
            found.append((start + base, 1, plane < extra, base))
        return found

    def piece(self, planes):
        return -(-max(self.halves) // planes)


def flip(plane, bit):
    one = plane + 1 - 2 * lax.rem(plane, 2)
    if isinstance(bit, int):
        return one if bit == 1 else lax.rem(plane + 2, 4)
    return one * (2 - bit) + lax.rem(plane + 2, 4) * (bit - 1)


def guarded(cond, action):
    if cond is None:
        action()
    else:
        pl.when(cond)(action)


def remote(src, dst, send, recv, peer):
    return pltpu.make_async_remote_copy(
        src_ref=src, dst_ref=dst, send_sem=send, recv_sem=recv, device_id=peer,
        device_id_type=MESH,
    )


def best_job(rows, columns, share=0.5):
    return Job(0 if rows % 16 == 0 else 1, rows, columns, 0, share)


class Engine:
    def both(self, action, *given):
        def run():
            core = self.core

            def at(which):
                def branch():
                    self.core = which
                    action(*given)
                return branch

            pl.when(core == 0)(at(0))
            pl.when(core != 0)(at(1))
            self.core = core

        return run


class Gather(Engine):
    def __init__(self, jobs, arrays, owners=None):
        self.jobs, self.arrays = jobs, arrays
        self.owners = owners or list(range(len(jobs)))
        planes, shards = sizes()
        count = len(jobs)
        dma = pltpu.SemaphoreType.DMA
        self.outs = [jax.ShapeDtypeStruct((shards,) + a.shape, a.dtype) for a in arrays]
        self.scratch = [
            dma((count, shards, 2, 2)), dma((count, shards, max(planes, 5), 2, 2)),
            dma((count, shards, 2)), dma((len(arrays), 2)),
        ] + [pltpu.VMEM(a.shape, a.dtype) for a in arrays]
        self.units = [(j, by) for j in range(count) for by in range(1, shards)]

    def bind(self, srcs, dsts, sems):
        self.all_srcs, self.all_dsts = srcs, dsts
        self.srcs = [srcs[n] for n in self.owners]
        self.dsts = [dsts[n] for n in self.owners]
        self.sem_z, self.sem_p, self.sem_c, self.sem_l = sems[:4]
        self.staged = sems[4:]
        self.plane, self.core, self.row, self.planes, self.shards = place()

    def mine(self, j, plane=None):
        job = self.jobs[j]
        plane = self.plane if plane is None else plane
        for i, (start, size, cond, _) in enumerate(job.parts(self.planes, plane, self.core)):
            yield i, start + job.starts[self.core] + job.first, size, cond

    def fetch(self, n):
        return pltpu.make_async_copy(self.all_srcs[n], self.staged[n], self.sem_l.at[n, 0])

    def local(self, n):
        return pltpu.make_async_copy(
            self.staged[n], self.all_dsts[n].at[self.row], self.sem_l.at[n, 1]
        )

    def turn(self, by):
        return by + self.core * (self.shards - 2 * by)

    def origin(self, by):
        return lax.rem(self.row + self.shards - by, self.shards)

    def copy_z(self, j, by, i, start, size, incoming):
        job = self.jobs[j]
        sems = self.sem_z.at[j, by, i, 0], self.sem_z.at[j, by, i, 1]
        peer = (self.plane * CORES + self.core, lax.rem(self.row + by, self.shards))
        if incoming:
            ref = job.cut(self.dsts[j].at[self.origin(by)], start, size)
            return remote(ref, ref, *sems, peer)
        src = job.cut(self.srcs[j], start, size)
        return remote(src, job.cut(self.dsts[j].at[self.row], start, size), *sems, peer)

    def half(self, ref, job, part):
        if job.axis:
            cut = -(-job.rows // 32) * 16
            return ref.at[pl.ds(0, cut)] if part == 0 else ref.at[pl.ds(cut, job.rows - cut)]
        cut = -(-job.columns // 256) * 128
        if part == 0:
            return ref.at[:, pl.ds(0, cut)]
        return ref.at[:, pl.ds(cut, job.columns - cut)]

    def copy_p(self, j, by, q, i, start, size):
        job = self.jobs[j]
        sems = self.sem_p.at[j, by, q, i, 0], self.sem_p.at[j, by, q, i, 1]
        ref = job.cut(self.dsts[j].at[self.origin(by)], start, size)
        if self.planes != 4:
            peer = plane_peer(self.plane, self.core, self.row, self.planes, q)
            return remote(ref, ref, *sems, peer)
        if q > 2:
            ref, q = self.half(ref, job, q - 3), q - 2
        return remote(ref, ref, *sems, (flip(self.plane, q) * CORES + self.core, self.row))

    def copy_c(self, j, by, core):
        job = self.jobs[j]
        start = job.starts[core] + job.first
        ref = job.cut(self.dsts[j].at[self.origin(by)], start, job.halves[core])
        peer = (self.plane * CORES + 1 - self.core, self.row)
        return remote(ref, ref, self.sem_c.at[j, by, 0], self.sem_c.at[j, by, 1], peer)

    def open(self):
        for n in range(len(self.arrays)):
            self.fetch(n).start()

    def keep(self):
        for n in range(len(self.arrays)):
            self.fetch(n).wait()
            self.local(n).start()

    def start(self, j, by):
        by = self.turn(by)
        for i, start, size, cond in self.mine(j):
            guarded(cond, lambda: self.copy_z(j, by, i, start, size, False).start())

    def by_core(self, first, second):
        @pl.when(self.core == 0)
        def _():
            first()
            second()

        @pl.when(self.core != 0)
        def _():
            second()
            first()

    def spread(self, j, by):
        by = self.turn(by)
        for i, start, size, cond in self.mine(j):
            def forward():
                self.copy_z(j, by, i, start, size, True).wait_recv()
                if self.planes == 4:
                    self.by_core(
                        self.copy_p(j, by, 1, i, start, size).start,
                        lambda: self.copy_p(j, by, 2, i, start, size).start(),
                    )
                else:
                    for q in range(1, self.planes):
                        self.copy_p(j, by, q, i, start, size).start()
            guarded(cond, forward)

    def relay(self, j, by):
        if self.planes != 4:
            return
        by = self.turn(by)

        def one(bit):
            def run():
                for i, start, size, cond in self.mine(j, plane=flip(self.plane, bit)):
                    def pass_on():
                        self.copy_p(j, by, bit, i, start, size).wait_recv()
                        self.copy_p(j, by, 5 - bit, i, start, size).start()
                    guarded(cond, pass_on)
            return run

        self.by_core(one(2), one(1))

    def across(self, j, by):
        by = self.turn(by)
        if self.planes == 4:
            for i, start, size, cond in self.mine(j, plane=flip(flip(self.plane, 1), 2)):
                def both():
                    for q in (3, 4):
                        self.copy_p(j, by, q, i, start, size).wait_recv()
                guarded(cond, both)
        else:
            for q in range(1, self.planes):
                origin = lax.rem(self.plane + self.planes - q, self.planes)
                for i, start, size, cond in self.mine(j, plane=origin):
                    guarded(cond, lambda: self.copy_p(j, by, q, i, start, size).wait_recv())
        self.copy_c(j, by, self.core).start()

    def arrived(self, j):
        for by in range(1, self.shards):
            self.copy_c(j, by, 1 - self.core).wait_recv()

    def close(self):
        for j, by in self.units:
            self.copy_c(j, by, self.core).wait_send()
            for i, start, size, cond in self.mine(j):
                def sent():
                    self.copy_z(j, by, i, start, size, False).wait_send()
                    for q in (1, 2) if self.planes == 4 else range(1, self.planes):
                        self.copy_p(j, by, q, i, start, size).wait_send()
                guarded(cond, sent)
            if self.planes == 4:
                for bit in (1, 2):
                    for i, start, size, cond in self.mine(j, plane=flip(self.plane, bit)):
                        guarded(
                            cond,
                            lambda: self.copy_p(j, by, 5 - bit, i, start, size).wait_send(),
                        )
        self.settle()

    def settle(self):
        for n in range(len(self.arrays)):
            self.local(n).wait()


class GatherHere(Gather):
    def __init__(self, jobs, arrays, owners):
        super().__init__(jobs, arrays, owners)
        self.scratch = self.scratch[:4]

    def local(self, n):
        return pltpu.make_async_copy(
            self.all_srcs[n], self.all_dsts[n].at[self.row], self.sem_l.at[n, 1]
        )

    def open(self):
        for n in range(len(self.arrays)):
            self.local(n).start()

    def keep(self):
        pass

    def settle(self):
        pass


class Reduce(Engine):
    def __init__(self, jobs, arrays, keep=True, near=0):
        self.jobs, self.arrays, self.keep, self.near = jobs, arrays, keep, near
        planes, shards = sizes()
        count = len(jobs)
        dma = pltpu.SemaphoreType.DMA
        low = jnp.bfloat16
        refs = []
        for job in jobs:
            piece = job.piece(planes)
            refs += [
                pltpu.VMEM((shards,) + job.shape(max(job.halves)), low),
                pltpu.VMEM((shards,) + job.shape(max(job.halves)), low),
                pltpu.VMEM((shards, planes - 1) + job.shape(piece), low),
                pltpu.VMEM((shards,) + job.shape(piece), low),
                pltpu.VMEM((shards - 1,) + job.shape(piece), low),
            ]
        self.outs = [
            jax.ShapeDtypeStruct(job.shape(job.piece(planes)), low) for job in jobs if keep
        ]
        self.scratch = refs + [
            dma((count, shards, 3)), dma((count, shards, planes, 2, 2)),
            dma((count, shards, 2, 2)), dma((count,)),
        ]
        self.units = [(j, s) for s in range(shards) for j in range(count)]

    def bind(self, grads, outs, refs):
        count = len(self.jobs)
        self.grads, self.fins = grads, outs
        self.bufs = [refs[5 * j : 5 * j + 5] for j in range(count)]
        self.sem_a, self.sem_b, self.sem_c, self.sem_f = refs[5 * count :]
        self.plane, self.core, self.row, self.planes, self.shards = place()

    def owner(self, s):
        return lax.rem(self.row + 1 + s, self.shards)

    def sibling(self):
        return (self.plane * CORES + 1 - self.core, self.row)

    def locate(self, j, s):
        return self.grads[j].at[self.owner(s)]

    def copy_a(self, j, s, core):
        job = self.jobs[j]
        src = job.cut(self.locate(j, s), job.starts[core], job.halves[core])
        dst = job.cut(self.bufs[j][1].at[s], 0, job.halves[core])
        return remote(
            src, dst, self.sem_a.at[j, s, 0], self.sem_a.at[j, s, 1], self.sibling()
        )

    def load_a(self, j, s):
        job = self.jobs[j]
        src = job.cut(self.locate(j, s), job.starts[self.core], job.halves[self.core])
        dst = job.cut(self.bufs[j][0].at[s], 0, job.halves[self.core])
        return pltpu.make_async_copy(src, dst, self.sem_a.at[j, s, 2])

    def copy_b(self, j, s, slot, peer, i, start, size, at):
        job = self.jobs[j]
        src = job.cut(self.bufs[j][0].at[s], start, size)
        dst = job.cut(self.bufs[j][2].at[s, slot], at, size)
        sems = self.sem_b.at[j, s, slot, i, 0], self.sem_b.at[j, s, slot, i, 1]
        return remote(src, dst, *sems, (peer * CORES + self.core, self.row))

    def sends(self, j, s, second):
        if self.planes != 4:
            return [] if second else [
                (
                    q - 1, lax.rem(self.plane + q, self.planes),
                    lax.rem(self.plane + q, self.planes),
                )
                for q in range(1, self.planes)
            ]
        near, far = self.order(j, s)
        if second:
            return [(2, flip(self.plane, far), flip(self.plane, far))]
        peer = flip(self.plane, near)
        return [(0, peer, peer), (1, peer, flip(peer, far))]

    def order(self, j, s):
        near = 2 - self.core if self.near else 1 + (j + s + self.core) % 2
        return near, 3 - near

    def copy_c(self, j, s, i, size, at):
        job = self.jobs[j]
        src = job.cut(self.bufs[j][3].at[s], at, size)
        dst = job.cut(self.bufs[j][4].at[s], at, size)
        peer = (self.plane * CORES + self.core, self.owner(s))
        return remote(src, dst, self.sem_c.at[j, s, i, 0], self.sem_c.at[j, s, i, 1], peer)

    def parts(self, j, plane):
        return enumerate(self.jobs[j].parts(self.planes, plane, self.core))

    def a_start(self, j, s):
        self.copy_a(j, s, 1 - self.core).start()
        self.load_a(j, s).start()

    def b_start(self, j, s):
        own, came = self.bufs[j][0], self.bufs[j][1]
        self.load_a(j, s).wait()
        self.copy_a(j, s, self.core).wait_recv()
        at = (s,) + self.jobs[j].index(0, self.jobs[j].halves[self.core])
        own[at] = (own[at].astype(jnp.float32) + came[at].astype(jnp.float32)).astype(own.dtype)
        self.b_send(j, s, False)

    def b_send(self, j, s, second):
        for slot, peer, piece in self.sends(j, s, second):
            for i, (start, size, cond, at) in self.parts(j, piece):
                guarded(
                    cond, lambda: self.copy_b(j, s, slot, peer, i, start, size, at).start()
                )

    def b_next(self, j, s):
        if self.planes != 4:
            return
        job = self.jobs[j]
        own, came = self.bufs[j][0], self.bufs[j][2]
        near, far = self.order(j, s)
        for slot, piece in ((0, self.plane), (1, flip(self.plane, far))):
            for i, (start, size, cond, at) in self.parts(j, piece):
                def add():
                    self.copy_b(
                        j, s, slot, flip(self.plane, near), i, start, size, at
                    ).wait_recv()
                    at_own = (s,) + job.index(start, size)
                    got = came[(s, slot) + job.index(at, size)].astype(jnp.float32)
                    own[at_own] = (own[at_own].astype(jnp.float32) + got).astype(own.dtype)
                guarded(cond, add)
        self.b_send(j, s, True)

    def c_start(self, j, s):
        job = self.jobs[j]
        own, came, piece = self.bufs[j][0], self.bufs[j][2], self.bufs[j][3]
        slots = [2] if self.planes == 4 else range(self.planes - 1)
        for i, (start, size, cond, at) in self.parts(j, self.plane):
            def add():
                total = own[(s,) + job.index(start, size)].astype(jnp.float32)
                for slot in slots:
                    self.copy_b(j, s, slot, self.plane, i, start, size, at).wait_recv()
                    total = total + came[(s, slot) + job.index(at, size)].astype(jnp.float32)
                piece[(s,) + job.index(at, size)] = total.astype(piece.dtype)
                if s < self.shards - 1:
                    self.copy_c(j, s, i, size, at).start()
            guarded(cond, add)

    def total(self, j):
        job = self.jobs[j]
        piece, came = self.bufs[j][3], self.bufs[j][4]
        final = self.shards - 1
        for i, (start, size, cond, at) in self.parts(j, self.plane):
            def add():
                total = piece[(final,) + job.index(at, size)].astype(jnp.float32)
                for s in range(final):
                    self.copy_c(j, s, i, size, at).wait_recv()
                    total = total + came[(s,) + job.index(at, size)].astype(jnp.float32)
                piece[(final,) + job.index(at, size)] = total.astype(piece.dtype)
            guarded(cond, add)
        if self.keep:
            self.copy_f(j).start()

    def copy_f(self, j):
        return pltpu.make_async_copy(
            self.bufs[j][3].at[self.shards - 1], self.fins[j], self.sem_f.at[j]
        )

    def finish(self, j):
        if self.keep:
            self.copy_f(j).wait()
        for s in range(self.shards):
            self.copy_a(j, s, 1 - self.core).wait_send()
            for slot, peer, piece in self.sends(j, s, False) + self.sends(j, s, True):
                for i, (start, size, cond, at) in self.parts(j, piece):
                    guarded(
                        cond,
                        lambda: self.copy_b(j, s, slot, peer, i, start, size, at).wait_send(),
                    )
        for i, (start, size, cond, at) in self.parts(j, self.plane):
            def sent():
                for s in range(self.shards - 1):
                    self.copy_c(j, s, i, size, at).wait_send()
            guarded(cond, sent)


class ReduceHere(Reduce):
    def locate(self, j, s):
        return self.grads[j].at[s] if j == 0 else self.grads[j].at[self.owner(s)]


class Share(Engine):
    def __init__(self, jobs, arrays, source=None):
        self.jobs, self.arrays, self.source = jobs, arrays, source
        planes, _ = sizes()
        count = len(jobs)
        dma = pltpu.SemaphoreType.DMA
        self.outs = [
            jax.ShapeDtypeStruct((job.rows, job.columns), jnp.bfloat16) for job in jobs
        ]
        self.scratch = [dma((count, planes, 2, 2)), dma((count, 2))]
        if source is None:
            self.scratch += [pltpu.VMEM(a.shape, a.dtype) for a in arrays] + [dma((count,))]

    def bind(self, fins, outs, sems):
        if self.source is not None:
            fins = [bufs[3].at[self.source.shards - 1] for bufs in self.source.bufs]
        self.given = fins
        self.fins, self.outs_ref = fins, outs
        self.sem_d, self.sem_e = sems[:2]
        if self.source is None:
            self.fins, self.sem_f = sems[2:-1], sems[-1]
        self.plane, self.core, self.row, self.planes, self.shards = place()

    def parts(self, j, plane):
        return enumerate(self.jobs[j].parts(self.planes, plane, self.core))

    def fetch(self, j):
        return pltpu.make_async_copy(self.given[j], self.fins[j], self.sem_f.at[j])

    def copy_d(self, j, q, i, start, size, at):
        job = self.jobs[j]
        src = job.cut(self.fins[j], at, size)
        dst = job.cut(self.outs_ref[j], start + job.starts[self.core], size)
        sems = self.sem_d.at[j, q, i, 0], self.sem_d.at[j, q, i, 1]
        if q == 0:
            return pltpu.make_async_copy(src, dst, sems[0])
        return remote(
            src, dst, *sems, plane_peer(self.plane, self.core, self.row, self.planes, q)
        )

    def copy_e(self, j, core):
        job = self.jobs[j]
        ref = job.cut(self.outs_ref[j], job.starts[core], job.halves[core])
        peer = (self.plane * CORES + 1 - self.core, self.row)
        return remote(ref, ref, self.sem_e.at[j, 0], self.sem_e.at[j, 1], peer)

    def start(self, j):
        if self.source is None:
            self.fetch(j).wait()
        for i, (start, size, cond, at) in self.parts(j, self.plane):
            def send():
                for q in range(self.planes):
                    self.copy_d(j, q, i, start, size, at).start()
            guarded(cond, send)

    def across(self, j):
        for q in range(1, self.planes):
            origin = lax.rem(self.plane + self.planes - q, self.planes)
            for i, (start, size, cond, at) in self.parts(j, origin):
                guarded(cond, lambda: self.copy_d(j, q, i, start, size, at).wait_recv())
        for i, (start, size, cond, at) in self.parts(j, self.plane):
            guarded(cond, lambda: self.copy_d(j, 0, i, start, size, at).wait())
        self.copy_e(j, self.core).start()

    def finish(self, j):
        self.copy_e(j, 1 - self.core).wait_recv()
        self.copy_e(j, self.core).wait_send()
        for i, (start, size, cond, at) in self.parts(j, self.plane):
            def sent():
                for q in range(1, self.planes):
                    self.copy_d(j, q, i, start, size, at).wait_send()
            guarded(cond, sent)


def any_spec():
    return pl.BlockSpec(memory_space=pl.ANY)


def sizes():
    return lax.axis_size("ctx") // CORES, lax.axis_size("fsdp")


def fused_call(
    kernel, steps, args, in_specs, out_specs, out_shape, scratch, engines, schedule, end, ident,
    chain=False, cost=None,
):
    n_in, n_out, n_scr = len(args), len(out_shape), len(scratch)
    e_in = [len(e.arrays) for e in engines]
    e_out = [len(e.outs) for e in engines]
    e_scr = [len(e.scratch) for e in engines]

    def cut(refs, first, counts):
        groups = [refs[:first]]
        for count in counts:
            groups.append(refs[first : first + count])
            first += count
        return groups, refs[first:]

    def kern(*refs):
        ins, refs = cut(refs, n_in, e_in)
        outs, refs = cut(refs, n_out, e_out)
        scrs, refs = cut(refs, n_scr, e_scr)
        for k, engine in enumerate(engines):
            engine.bind(ins[k + 1], outs[k + 1], scrs[k + 1])
        step = pl.program_id(0)
        pl.when(step == 0)(lambda: greet(chain))
        for when in sorted(schedule):
            def act():
                for action in schedule[when]:
                    action()
            pl.when(step == when)(act)
        if kernel is not None:
            kernel(*ins[0], *outs[0], *scrs[0])
        def close():
            for action in end:
                action()
        pl.when(step == steps - 1)(close)

    flat = lambda groups: [item for group in groups for item in group]
    found = pl.pallas_call(
        kern,
        grid=(steps,),
        in_specs=list(in_specs) + [any_spec()] * sum(e_in),
        out_specs=list(out_specs) + [any_spec()] * sum(e_out),
        out_shape=list(out_shape) + flat([e.outs for e in engines]),
        scratch_shapes=list(scratch) + flat([e.scratch for e in engines]),
        compiler_params=pltpu.CompilerParams(
            vmem_limit_bytes=VMEM_BYTES, collective_id=ident, has_side_effects=True,
            fuse_transposed_lhs_in_matmul=True,
        ),
        cost_estimate=cost,
    )(*args, *flat([e.arrays for e in engines]))
    groups, _ = cut(found, n_out, e_out)
    return groups


def call(action, *given):
    return lambda: action(*given)


class HaloBack:
    def __init__(self, pairs, wide):
        self.arrays = []
        self.pairs = pairs
        dma = pltpu.SemaphoreType.DMA
        self.outs = [jax.ShapeDtypeStruct((2 * pairs, WINDOW, TILE), jnp.bfloat16)]
        self.scratch = [
            pltpu.VMEM((pairs, 2, WINDOW, TILE), jnp.bfloat16), dma((pairs, 2, 2)),
        ]

    def bind(self, _, outs, refs):
        (self.out,), (self.buf, self.sems) = outs, refs
        self.ctx, self.row = lax.axis_index("ctx"), lax.axis_index("fsdp")
        self.last = lax.axis_size("ctx") - 1

    def copy(self, pair, side):
        return remote(
            self.buf.at[pair, side], self.out.at[side * self.pairs + pair],
            self.sems.at[pair, side, 0], self.sems.at[pair, side, 1],
            (jnp.maximum(self.ctx - 1, 0), self.row),
        )

    def send(self, pair):
        @pl.when(self.ctx > 0)
        def _():
            for side in range(2):
                self.copy(pair, side).start()

    def finish(self):
        @pl.when(self.ctx > 0)
        def _():
            for pair in range(self.pairs):
                for side in range(2):
                    self.copy(pair, side).wait_send()

        @pl.when(self.ctx < self.last)
        def _():
            for pair in range(self.pairs):
                for side in range(2):
                    self.copy(pair, side).wait_recv()


class Small:
    def __init__(self, array):
        self.arrays = [array]
        planes, shards = sizes()
        dma = pltpu.SemaphoreType.DMA
        self.outs = [jax.ShapeDtypeStruct(array.shape, jnp.float32)]
        self.peers = 1, planes - 1, shards - 1
        self.scratch = [
            pltpu.VMEM((4,) + array.shape, jnp.float32),
            pltpu.VMEM((sum(self.peers),) + array.shape, jnp.float32),
            dma((sum(self.peers), 2)), dma((2,)),
        ]

    def bind(self, given, outs, refs):
        (self.given,), (self.out,) = given, outs
        self.own, self.came, self.sems, self.sem_l = refs
        self.plane, self.core, self.row, self.planes, self.shards = place()

    def load(self):
        return pltpu.make_async_copy(self.given, self.own.at[0], self.sem_l.at[0])

    def save(self):
        return pltpu.make_async_copy(self.own.at[3], self.out, self.sem_l.at[1])

    def copy(self, stage, n):
        at = sum(self.peers[:stage]) + n
        if stage == 0:
            peer = (self.plane * CORES + 1 - self.core, self.row)
        elif stage == 1:
            peer = plane_peer(self.plane, self.core, self.row, self.planes, n + 1)
        else:
            peer = (self.plane * CORES + self.core, lax.rem(self.row + n + 1, self.shards))
        return remote(
            self.own.at[stage], self.came.at[at], self.sems.at[at, 0], self.sems.at[at, 1], peer
        )

    def send(self, stage):
        for n in range(self.peers[stage]):
            self.copy(stage, n).start()

    def add(self, stage):
        total = self.own[stage]
        for n in range(self.peers[stage]):
            self.copy(stage, n).wait_recv()
            total = total + self.came[sum(self.peers[:stage]) + n]
        self.own[stage + 1] = total

    def finish(self):
        self.save().start()
        for stage in range(3):
            for n in range(self.peers[stage]):
                self.copy(stage, n).wait_send()
        self.save().wait()


def layer_norm(values, gain, shift):
    middle = jnp.mean(values, axis=-1, keepdims=True)
    centred = values - middle
    spread = jnp.mean(centred * centred, axis=-1, keepdims=True)
    return centred * lax.rsqrt(spread + epsilon) * gain + shift


def passed_along(value, axis, by):
    peers = lax.axis_size(axis)
    pairs = [(i, i + by) for i in range(peers) if 0 <= i + by < peers]
    return lax.ppermute(value, axis, pairs)


def segment_ids(lengths_row, positions):
    ends = jnp.cumsum(lengths_row)
    found = jnp.sum((positions[:, None] >= ends[None, :]).astype(jnp.int32), axis=1)
    return jnp.where(positions >= 0, found, -1)


def padded(array, parts):
    rows, columns = array.shape
    each = columns // parts
    wide = -(-each // TILE) * TILE
    array = array.reshape(rows, parts, each)
    return jnp.pad(array, ((0, 0), (0, 0), (0, wide - each))).reshape(rows, parts * wide)


def widened(array, columns):
    return jnp.pad(array, ((0, 0), (0, columns - array.shape[1])))


def even(columns):
    return -(-columns // (CORES * TILE)) * CORES * TILE


def on_device(
    activations, doc_lengths, cotangent, attn_gain, attn_shift, w_qkv, query_bias, value_bias,
    w_out, out_bias, mlp_gain, mlp_shift, w_fc, fc_bias, w_proj, proj_bias,
):
    low = jnp.bfloat16
    shards = lax.axis_size("fsdp")
    shard_rows, hidden = w_fc.shape
    features = activations.shape[2]
    wide = -(-features // TILE) * TILE
    pairs = wide // TILE
    qkv_wide, out_wide = even(3 * wide), even(features)
    own_hidden = w_proj.shape[0]
    first = own_hidden * 8 // 17
    second = own_hidden - first
    job_qkv, job_out = best_job(shard_rows, qkv_wide), best_job(shard_rows, out_wide)
    jobs_a = [best_job(shard_rows, shards * first), Job(0, first, features)]
    jobs_b = [best_job(shard_rows, shards * second), Job(0, second, features)]
    uneven_b = [
        best_job(shard_rows, shards * second, 0.35), Job(0, second, features, 0, 0.35)
    ]

    x_t, cot_t = activations[0].T, cotangent[0].T
    tok = x_t.shape[1]
    vectors = (
        attn_gain, attn_shift, query_bias, value_bias, out_bias, mlp_gain, mlp_shift, proj_bias,
    )
    vec = jnp.concatenate([v[None] for v in vectors] + [fc_bias.reshape(-1, shard_rows)])
    vec = jnp.pad(vec, ((0, 2 * TILE - vec.shape[0]), (0, 0))).T
    (
        qkv, halo, normed1_t, cot, vfull, qkv_w, fc_a, fc_b, proj_a, proj_b, out_low,
    ) = first_call(
        x_t, cot_t, w_qkv, vec, w_fc, w_proj, w_out, first, wide, qkv_wide, out_wide, 0
    )
    qkv_w = qkv_w.reshape(features, qkv_wide)
    vfull = vfull[:, :, :TILE].astype(jnp.float32)
    gain_one = vfull[:, :, 0].reshape(features, 1)
    vec_two = jnp.stack([vfull[:, :, n].reshape(-1) for n in (4, 5, 6, 7)])
    pbias = vec_two[3:4]
    fcbias = vfull[:, :, 8 : 8 + own_hidden // shard_rows].transpose(0, 2, 1)
    fcbias = fcbias.reshape(shards, own_hidden)

    first_pos = lax.axis_index("ctx") * tok
    ext_positions = first_pos - WINDOW + jnp.arange(tok + WINDOW, dtype=jnp.int32)
    doc_ext = segment_ids(doc_lengths[0], ext_positions)
    ids = jnp.arange(TILE, dtype=jnp.int32)[None, :]
    same = doc_ext[:, None] == ids
    qdoc = same[WINDOW:].astype(low)
    kdoc = jnp.where(same | (ids >= doc_lengths.shape[1]), 0.0, masked_score).astype(low)

    (attended, full, stat), (out_w, fc_wa, proj_wa) = attention_forward(
        qkv, halo, qdoc, kdoc, features,
        Gather([job_out] + jobs_a, [out_low, fc_a, proj_a]),
        1,
    )
    out_w = out_w.reshape(features, out_wide)
    lse = stat.T[: 2 * pairs].reshape(pairs, 2, tok)
    fcb_a = fcbias[:, :first].reshape(1, -1)
    fcb_b = fcbias[:, first:].reshape(1, -1)
    rest = Gather(jobs_b, [fc_b, proj_b])
    (
        (base, dnorm_a, gproj_a, gfc_a, gfcb_a, resid, normed2_low, normed2_t), (fc_wb, proj_wb),
    ) = mlp_part(
        (attended, out_w, x_t, vec_two), None, cot, cot_t, None, None, None,
        fc_wa.reshape(features, -1), fcb_a, proj_wa.reshape(-1, features),
        rest, *gather_plan(rest, shards * first // 256), 2,
    )
    sum_a = Reduce(
        jobs_a,
        [gfc_a.reshape(shards, shard_rows, -1), gproj_a.reshape(shards, first, features)],
    )
    schedule, end, done = reduce_plan(sum_a, shards * second // 256, shards * second // 256 - 3)
    (block_out, dnormed2, gproj_b, gfc_b, gfcb_b), fins_a = mlp_part(
        normed2_low, normed2_t, cot, cot_t, base, dnorm_a, pbias,
        fc_wb.reshape(features, -1), fcb_b, proj_wb.reshape(-1, features),
        sum_a, schedule, end + done, 3,
    )
    (gresid_t, grad_attended, grad_wout, mid_sums), (r_fca, r_proja) = middle(
        dnormed2, resid, cot, attended, out_w, vec_two, Share(jobs_a, fins_a), 6
    )
    sum_b = Reduce(
        uneven_b,
        [gfc_b.reshape(shards, shard_rows, -1), gproj_b.reshape(shards, second, features)],
        near=2,
    )
    (dq, dko, dvo), fins_b, (back,) = attention_backward(
        qkv, halo, grad_attended, full, lse, qdoc, kdoc, features, sum_b, 4
    )
    small = jnp.concatenate([
        jnp.zeros((4, features), jnp.float32),
        jnp.stack([mid_sums[2], mid_sums[0], mid_sums[1], mid_sums[3]]),
        jnp.concatenate(
            [gfcb_a.reshape(shards, first), gfcb_b.reshape(shards, second)], axis=1
        ).reshape(-1, features),
    ])
    small = jnp.pad(small, ((0, -small.shape[0] % 8), (0, 0)))
    input_grad_t, r_qkv, r_out, r_fcb, r_projb, small = last_call(
        [job_qkv, job_out], Share(uneven_b, fins_b), normed1_t, x_t, gain_one, dq, dko, dvo, back, qkv_w, gresid_t,
        grad_wout.reshape(shards, shard_rows, out_wide), small, 5,
    )
    r_qkv, r_out, r_fc, block_out, input_grad_t, r_proj = finals(
        features, shards, r_qkv, r_out, r_fca, r_fcb, block_out, input_grad_t, r_proja, r_projb
    )
    row = lax.axis_index("fsdp")
    sums = [
        lax.dynamic_slice_in_dim(small[n], row * shard_rows, shard_rows) for n in range(8)
    ]
    fcb_sum = lax.dynamic_slice_in_dim(
        small[8 : 8 + hidden // features].reshape(-1), row * own_hidden, own_hidden
    )
    return (
        block_out.T[None], input_grad_t.T[None], sums[0], sums[1], r_qkv, sums[2], sums[3], r_out,
        sums[4], sums[5], sums[6], r_fc, fcb_sum, r_proj, sums[7],
    )


def solution(mesh):
    vec, mat = P("fsdp"), P("fsdp", None)
    seq = P("fsdp", "ctx", None)
    placed = (
        seq, mat, seq, vec, vec, mat, vec, vec, mat, vec, vec, vec, mat, vec, mat, vec,
    )
    return jax.shard_map(
        on_device,
        mesh=mesh,
        in_specs=placed,
        out_specs=(seq, seq, vec, vec, mat, vec, vec, mat, vec, vec, vec, mat, vec, mat, vec),
        check_vma=False,
    )
```
